1024 devices in a mesh: gx: 16 (over y_hi, z), gy: 64 (over y_lo, x, core).
Axes of the slice: x: 8, y: 8 (y_hi: 2, y_lo: 4; y = y_hi * 4 + y_lo), z: 8, core: 2. Of those that a mesh axis runs over, the one named last changes fastest.
Arguments:
- air_state: float32 [512, 2048, 128], P('gx', 'gy'), may hold values from -3 to 4, as said below
- edge_map: int32 [16, 64, 4], replicated, may hold values from 0 to 7
- tile_class: int32 [16, 64, 16], P(None, 'gy'), may hold values from 0 to 1, as said below
- in_weight: bfloat16 [128, 1024], replicated, may hold values from -0.5 to 0.5
- in_bias: float32 [1024], replicated, may hold values from -4 to 4
- mid_weight: bfloat16 [1024, 1024], replicated, may hold values from -0.1875 to 0.1875
- mid_bias: float32 [1024], replicated, may hold values from -4 to 4
- out_weight: bfloat16 [1024, 128], replicated, may hold values from -0.1875 to 0.1875
- land_in: bfloat16 [128, 1024], replicated, may hold values from -0.5 to 0.5
- land_bias: float32 [1024], replicated, may hold values from -4 to 4
- land_out: bfloat16 [1024, 128], replicated, may hold values from -0.1875 to 0.1875
Outputs:
- tendency: float32 [512, 2048, 128], P('gx', 'gy')
The draws below stay inside these ranges and needn't reach their ends.
Inputs may be any that keep to these rules, and one draw needn't show every extreme that they name: `air_state`: density lies in 0.5 to 2, the speeds (momentum over density) are at most 1.5 in magnitude and potential temperature lies in 0.5 to 2. For every gy index g and tile number t, exactly 4 of the devices d along gx have tile_class[d, g, t] = 1.
All inputs are finite; a program needn't handle non-finite values.
Results may differ from the reference program's by a relative error of at most 0.0024.
Values may be sent and summed in bfloat16 or wider, within the bound.
No kernel may reach another device: no remote copies, remote signals or barrier semaphores. Data moves between devices by JAX's collectives and lax.ppermute only.
A program may use at most 64 MiB of HBM per device.

```python
import math
import jax
import jax.numpy as jnp
import numpy as np
from jax import lax

LEV = 32
HID = 1024
LAND_HID = 1024
FEAT = 128
NODES = 32
TILE_COLS = 64
LAND_TILES = 4
NXN = 512
NYN = 2048
N_GX = 16
N_GY = 64


def draw_air_state(key, part):
    key = jax.random.fold_in(key, 11)
    key_density, key_first, key_second, key_theta = jax.random.split(key, 4)
    shape = (NXN, NYN, LEV)
    density = jnp.exp(jax.random.uniform(key_density, shape, jnp.float32, math.log(0.5), math.log(2.0)))
    first_speed = jax.random.uniform(key_first, shape, jnp.float32, -1.0, 1.0)
    second_speed = jax.random.uniform(key_second, shape, jnp.float32, -1.0, 1.0)
    theta = jax.random.uniform(key_theta, shape, jnp.float32, 0.5, 2.0)
    return jnp.concatenate([density, density * first_speed, density * second_speed, density * theta], axis=-1)


def draw_tile_class(key, part):
    key = jax.random.fold_in(key, 5)
    spread_width = max(2, N_GX // 4)
    offsets = jax.random.randint(key, (N_GY, N_GX), 0, spread_width + 1)
    devices = jnp.arange(N_GX, dtype=jnp.int32)[:, None, None]
    landed = (devices - offsets[None]) % N_GX < LAND_TILES
    return landed.astype(jnp.int32)


def touch_ends(values, own_key, smallest, largest):
    shape = values.shape
    index_at = [jax.random.randint(jax.random.fold_in(own_key, axis), (), 0, shape[axis]) for axis in range(len(shape))]
    values = values.at[tuple(index_at)].set(smallest)
    longest = shape.index(max(shape))
    index_at[longest] = (index_at[longest] + 1) % shape[longest]
    return values.at[tuple(index_at)].set(largest)


def scatter_about(stream_key, extent, spread, limit, kind=jnp.bfloat16):
    values = spread * jax.random.normal(stream_key, extent, jnp.float32)
    return jnp.clip(values, min=-limit, max=limit).astype(kind)


def setup_inputs(seed: int = 0) -> dict:
    splits = jax.random.split(jax.random.key(seed), 12)
    air_state = draw_air_state(jax.random.fold_in(splits[11], 71), 0)
    edge_map = touch_ends(jax.random.randint(splits[1], (N_GX, N_GY, 4), 0, 8), jax.random.fold_in(splits[1], 1), 0, 7).astype(jnp.int32)
    tile_class = draw_tile_class(jax.random.fold_in(splits[11], 71), 0)
    in_weight = scatter_about(splits[3], (FEAT, HID), FEAT ** -0.5, 0.5)
    in_bias = scatter_about(splits[4], (HID,), 1.0, 4.0, jnp.float32)
    mid_weight = scatter_about(splits[5], (LAND_HID, LAND_HID), LAND_HID ** -0.5, 0.1875)
    mid_bias = scatter_about(splits[6], (LAND_HID,), 1.0, 4.0, jnp.float32)
    out_weight = scatter_about(splits[7], (HID, FEAT), HID ** -0.5, 0.1875)
    land_in = scatter_about(splits[8], (FEAT, LAND_HID), FEAT ** -0.5, 0.5)
    land_bias = scatter_about(splits[9], (LAND_HID,), 1.0, 4.0, jnp.float32)
    land_out = scatter_about(splits[10], (LAND_HID, FEAT), LAND_HID ** -0.5, 0.1875)
    return {"air_state": air_state, "edge_map": edge_map, "tile_class": tile_class, "in_weight": in_weight, "in_bias": in_bias, "mid_weight": mid_weight, "mid_bias": mid_bias, "out_weight": out_weight, "land_in": land_in, "land_bias": land_bias, "land_out": land_out}


def lobatto_tables():
    points = np.array([-1.0, -math.sqrt(0.2), math.sqrt(0.2), 1.0])
    weights = [1.0 / 6.0, 5.0 / 6.0, 5.0 / 6.0, 1.0 / 6.0]
    barycentric = np.array([1.0 / np.prod([points[j] - points[k] for k in range(4) if k != j]) for j in range(4)])
    derivative = np.zeros((4, 4))
    for i in range(4):
        for j in range(4):
            if i != j:
                derivative[i, j] = barycentric[j] / barycentric[i] / (points[i] - points[j])
        derivative[i, i] = -np.sum([derivative[i, k] for k in range(4) if k != i])
    return (derivative, weights)

def primitives(states, direction):
    levels = states.shape[-1] // 4
    density = states[..., :levels]
    density_all = jnp.concatenate([density] * 4, axis=-1)
    carried = states / density_all
    velocity = carried[..., direction * levels:(direction + 1) * levels]
    velocity_all = jnp.concatenate([velocity] * 4, axis=-1)
    pressure = 0.5 * states[..., 3 * levels:]
    zero_block = jnp.zeros_like(pressure)
    pieces = [zero_block, zero_block, zero_block, zero_block]
    pieces[direction] = pressure
    pressure_all = jnp.concatenate(pieces, axis=-1)
    return (density_all, velocity_all, carried, pressure_all)

def two_point(state_one, state_two):
    return 0.125 * (state_one[0] + state_two[0]) * (state_one[1] + state_two[1]) * (state_one[2] + state_two[2]) + 0.5 * (state_one[3] + state_two[3])

def directional(states, low_trace, high_trace, direction):
    derivative, weights = lobatto_tables()
    node_count, cross_count, features = states.shape
    elements = node_count // 4
    blocked = states.reshape(elements, 4, cross_count, features)
    node_prims = [primitives(blocked[:, a], direction) for a in range(4)]
    left_states = jnp.concatenate([low_trace[None], blocked[:, 3]], axis=0)
    right_states = jnp.concatenate([blocked[:, 0], high_trace[None]], axis=0)
    left_prims = primitives(left_states, direction)
    right_prims = primitives(right_states, direction)
    wave_speed = jnp.maximum(jnp.abs(left_prims[1]), jnp.abs(right_prims[1])) + 1.0
    face_flux = two_point(left_prims, right_prims) - 0.5 * wave_speed * (right_states - left_states)
    pair_flux = {}
    for a in range(4):
        for b in range(a, 4):
            pair_flux[a, b] = two_point(node_prims[a], node_prims[b])
    results = []
    for a in range(4):
        volume = jnp.zeros_like(pair_flux[0, 0])
        for b in range(4):
            key_pair = (a, b) if a <= b else (b, a)
            volume = volume + 2.0 * float(derivative[a, b]) * pair_flux[key_pair]
        result = -volume
        if a == 0:
            result = result + 1.0 / weights[0] * (face_flux[:-1] - pair_flux[0, 0])
        if a == 3:
            result = result - 1.0 / weights[3] * (face_flux[1:] - pair_flux[3, 3])
        results.append(result)
    return jnp.stack(results, axis=1).reshape(node_count, cross_count, features)

def device_dynamics(block, west_trace, east_trace, south_trace, north_trace):
    along_first = directional(block, west_trace, east_trace, 1)
    along_second = directional(block.transpose(1, 0, 2), south_trace, north_trace, 2).transpose(1, 0, 2)
    return along_first + along_second

def normalize(columns):
    values = columns.astype(jnp.float32)
    inverse_rms = lax.rsqrt(lax.optimization_barrier(jnp.mean(values * values, axis=-1, keepdims=True)) + 1e-06)
    return (values * inverse_rms).astype(jnp.bfloat16)

def main_branch(normed, in_weight, in_bias, out_weight):
    first_hidden = jax.nn.silu(jnp.dot(normed, in_weight, preferred_element_type=jnp.float32) + in_bias).astype(jnp.bfloat16)
    return jnp.dot(first_hidden, out_weight, preferred_element_type=jnp.float32)

def land_branch(normed, land_in, land_bias, mid_weight, mid_bias, land_out):
    land_hidden = jax.nn.silu(jnp.dot(normed, land_in, preferred_element_type=jnp.float32) + land_bias).astype(jnp.bfloat16)
    land_second = jax.nn.silu(jnp.dot(land_hidden, mid_weight, preferred_element_type=jnp.float32) + mid_bias).astype(jnp.bfloat16)
    return jnp.dot(land_second, land_out, preferred_element_type=jnp.float32)

def reference(air_state, edge_map, tile_class, in_weight, in_bias, mid_weight, mid_bias, out_weight, land_in, land_bias, land_out):
    blocks = air_state.reshape(N_GX, NODES, N_GY, NODES, FEAT)
    side_edges = [blocks[:, 0], blocks[:, -1], blocks[:, :, :, 0].transpose(0, 2, 1, 3), blocks[:, :, :, -1].transpose(0, 2, 1, 3)]
    every_edge = jnp.stack(side_edges, axis=2)
    neighbours = [jnp.roll(every_edge, 1, axis=0), jnp.roll(every_edge, -1, axis=0), jnp.roll(every_edge, 1, axis=1), jnp.roll(every_edge, -1, axis=1)]
    partners = []
    for s in range(4):
        edge_codes = edge_map[:, :, s]
        chosen = jnp.take_along_axis(neighbours[s], (edge_codes % 4).astype(jnp.int32)[:, :, None, None, None], axis=2)[:, :, 0]
        partners.append(jnp.where((edge_codes >= 4)[:, :, None, None], chosen[:, :, ::-1], chosen))
    device_blocks = blocks.transpose(2, 0, 1, 3, 4)
    partner_stack = jnp.stack(partners, axis=0).transpose(2, 0, 1, 3, 4)
    classes = tile_class.transpose(1, 0, 2)

    def one_row(row_items):
        block_row, partner_row, class_row = row_items
        dynamics = jax.vmap(device_dynamics)(block_row, partner_row[0], partner_row[1], partner_row[2], partner_row[3])
        columns = block_row.reshape(N_GX * NODES * NODES, FEAT).astype(jnp.bfloat16)
        normed = normalize(columns)
        base_term = main_branch(normed, in_weight, in_bias, out_weight)
        land_term = land_branch(normed, land_in, land_bias, mid_weight, mid_bias, land_out)
        land_weight = jnp.repeat(class_row.reshape(-1), TILE_COLS).astype(jnp.float32)[:, None]
        physics = (base_term + land_weight * land_term).astype(jnp.bfloat16)
        return dynamics + physics.astype(jnp.float32).reshape(N_GX, NODES, NODES, FEAT)
    row_results = lax.map(one_row, (device_blocks, partner_stack, classes))
    return row_results.transpose(1, 2, 0, 3, 4).reshape(N_GX * NODES, N_GY * NODES, FEAT)
```

```python
import math

import jax
import jax.numpy as jnp
import numpy as np
from jax import lax
from jax.experimental import pallas as pl
from jax.experimental.pallas import tpu as pltpu
from jax.sharding import PartitionSpec as P

CHUNK = 8
FIRST, SECOND = "first", "second"


def lobatto_derivative():
    points = np.array([-1.0, -math.sqrt(0.2), math.sqrt(0.2), 1.0])
    barycentric = np.array(
        [1.0 / np.prod([points[j] - points[k] for k in range(4) if k != j]) for j in range(4)]
    )
    derivative = np.zeros((4, 4))
    for i in range(4):
        for j in range(4):
            if i != j:
                derivative[i, j] = barycentric[j] / barycentric[i] / (points[i] - points[j])
        derivative[i, i] = -np.sum([derivative[i, k] for k in range(4) if k != i])
    return derivative


def lane_block(shape):
    return lax.broadcasted_iota(jnp.int32, shape, len(shape) - 1) // 32


def spread(values, block, source):
    axis = values.ndim - 1
    if source == 0:
        once = jnp.where(block == 0, values, pltpu.roll(values, 32, axis))
        return jnp.where(block < 2, once, pltpu.roll(once, 64, axis))
    if source == 1:
        once = jnp.where(block == 1, values, pltpu.roll(values, 96, axis))
        return jnp.where(block < 2, once, pltpu.roll(once, 64, axis))
    once = jnp.where(block == 2, values, pltpu.roll(values, 32, axis))
    return jnp.where(block >= 2, once, pltpu.roll(once, 64, axis))


def primitives(states):
    flat = states.reshape(-1, states.shape[-1])
    block = lane_block(flat.shape)
    density = spread(flat, block, 0)
    carried = flat / density
    first = spread(carried, block, 1)
    second = spread(carried, block, 2)
    carried = jnp.where(block == 0, 1.0, carried)
    half_pressure = 0.25 * flat
    zero = jnp.zeros_like(flat)
    pressure_first = jnp.where(block == 1, pltpu.roll(half_pressure, 64, 1), zero)
    pressure_second = jnp.where(block == 2, pltpu.roll(half_pressure, 96, 1), zero)
    back = lambda x: x.reshape(states.shape)
    return {
        "q": states,
        "d": back(density),
        "c": back(carried),
        FIRST: (back(0.125 * first), back(pressure_first)),
        SECOND: (back(0.125 * second), back(pressure_second)),
    }


def pick(prims, index):
    out = {k: prims[k][index] for k in ("q", "d", "c")}
    for k in (FIRST, SECOND):
        out[k] = tuple(x[index] for x in prims[k])
    return out


def flux(one, two, axis):
    return (one["d"] + two["d"]) * (one[axis][0] + two[axis][0]) * (one["c"] + two["c"]) + (
        one[axis][1] + two[axis][1]
    )


def face(left, right, axis):
    wave = 8.0 * jnp.maximum(jnp.abs(left[axis][0]), jnp.abs(right[axis][0])) + 1.0
    return 6.0 * flux(left, right, axis) - (3.0 * wave) * (right["q"] - left["q"])


def volume(nodes, axis):
    derivative = lobatto_derivative()
    fluxes = {}
    for a in range(4):
        for b in range(a + 1, 4):
            fluxes[a, b] = fluxes[b, a] = flux(nodes[a], nodes[b], axis)
    results = []
    for a in range(4):
        total = None
        for b in range(4):
            if b != a:
                term = (-2.0 * float(derivative[a, b])) * fluxes[a, b]
                total = term if total is None else total + term
        results.append(total)
    return results


def silu(z):
    half = 0.5 * z
    return (half + half * jnp.tanh(half)).astype(jnp.bfloat16)


def dot(a, b):
    return jnp.dot(a, b, preferred_element_type=jnp.float32)


def main_kernel(
    air, classes, edge_map, in_w, in_b, mid_w, mid_b, out_w, land_in, land_b, land_out, out, codes
):
    rows, cols, feat = air.shape
    elements = cols // 4
    device_row = lax.axis_index("gx")
    device_col = lax.axis_index("gy")
    for s in range(4):
        codes[s] = edge_map[device_row, s, device_col]

    def chunk(c, carry):
        base_row = pl.multiple_of(c * CHUNK, CHUNK)
        columns = air[pl.ds(base_row, CHUNK)].reshape(CHUNK * cols, feat).astype(jnp.bfloat16)
        values = columns.astype(jnp.float32)
        mean = jnp.sum(values * values, axis=-1, keepdims=True) * (1.0 / feat)
        normed = (values * lax.rsqrt(mean + 1e-06)).astype(jnp.bfloat16)
        hidden = silu(dot(normed, in_w[...]) + in_b[...])
        total = dot(hidden, out_w[...])
        land = silu(dot(normed, land_in[...]) + land_b[...])
        land = silu(dot(land, mid_w[...]) + mid_b[...])
        land_term = dot(land, land_out[...])
        tiles = CHUNK * cols // 64
        pieces = []
        for t in range(tiles):
            weight = classes[device_row, 0, c * tiles + t].astype(jnp.float32)
            cut = slice(t * 64, (t + 1) * 64)
            pieces.append(total[cut] + weight * land_term[cut])
        physics = jnp.concatenate(pieces, axis=0).astype(jnp.bfloat16).astype(jnp.float32)
        out[pl.ds(base_row, CHUNK)] = physics.reshape(CHUNK, cols, feat)

        before = jnp.maximum(base_row - 1, 0)
        after = jnp.minimum(base_row + CHUNK, rows - 1)
        has_before = jnp.where(c > 0, 1.0, 0.0)
        has_after = jnp.where(c < rows // CHUNK - 1, 1.0, 0.0)
        seconds = []
        for a in range(4):
            along = pl.ds(a, elements, stride=4)
            states = air[pl.ds(base_row, CHUNK), along, :]
            prims = primitives(states)
            seconds.append(prims)
            low = primitives(air[pl.ds(before, 1), along, :])
            high = primitives(air[pl.ds(after, 1), along, :])
            result = [None] * CHUNK
            faces = []
            count = CHUNK // 4
            for e in range(count):
                nodes = [pick(prims, slice(e * 4 + k, e * 4 + k + 1)) for k in range(4)]
                if e == 0:
                    faces.append(face(low, nodes[0], FIRST) * has_before)
                else:
                    faces.append(face(last, nodes[0], FIRST))
                last = nodes[3]
                vol = volume(nodes, FIRST)
                for k in range(4):
                    result[e * 4 + k] = vol[k]
            faces.append(face(last, high, FIRST) * has_after)
            for e in range(count):
                result[e * 4] = result[e * 4] + faces[e]
                result[e * 4 + 3] = result[e * 4 + 3] - faces[e + 1]
            for k in range(CHUNK):
                place = (pl.ds(base_row + k, 1), along, slice(None))
                out[place] = out[place] + result[k]
        vol = volume(seconds, SECOND)
        shape = (CHUNK, elements, feat)
        low_nodes = jax.tree.map(lambda x: pltpu.roll(x, 1, 1), seconds[3])
        faces = face(low_nodes, seconds[0], SECOND)
        faces = jnp.where(lax.broadcasted_iota(jnp.int32, shape, 1) == 0, 0.0, faces)
        vol[0] = vol[0] + faces
        vol[3] = vol[3] - pltpu.roll(faces, elements - 1, 1)
        for a in range(4):
            place = (pl.ds(base_row, CHUNK), pl.ds(a, elements, stride=4), slice(None))
            out[place] = out[place] + vol[a]
        return carry

    lax.fori_loop(0, rows // CHUNK, chunk, 0)


def oriented(candidates, code):
    chosen = candidates[code % 4]
    count = chosen.shape[0] // 8
    place = lax.broadcasted_iota(jnp.int32, (8, chosen.shape[1]), 0)
    turned = []
    for k in range(count):
        piece = chosen[(count - 1 - k) * 8 : (count - k) * 8]
        piece = pltpu.roll(piece, 4, 0)
        piece = jnp.where(place % 4 < 2, pltpu.roll(piece, 6, 0), pltpu.roll(piece, 2, 0))
        piece = jnp.where(place % 2 < 1, pltpu.roll(piece, 7, 0), pltpu.roll(piece, 1, 0))
        turned.append(piece)
    return jnp.where(code >= 4, jnp.concatenate(turned, axis=0), chosen)


def edge_kernel(
    codes, edges, west, east, south, north, partial, out, low, high, top, bottom, sems
):
    rows, cols, feat = out.shape
    first, middle, final = pl.ds(0, 8), pl.ds(8, cols - 16), pl.ds(cols - 8, 8)
    places = [
        (low, (slice(None), first)),
        (high, (slice(None), final)),
        (top, (0, middle)),
        (bottom, (rows - 1, middle)),
    ]
    reads = [
        pltpu.make_async_copy(partial.at[p], held, sems.at[k])
        for k, (held, p) in enumerate(places)
    ]
    for copy in reads:
        copy.start()
    own = [primitives(edges[s]) for s in range(4)]
    others = [
        primitives(oriented(ref, codes[s])) for s, ref in enumerate((west, east, south, north))
    ]
    at_west = face(others[0], own[0], FIRST)
    at_east = -face(own[1], others[1], FIRST)
    at_south = face(others[2], own[2], SECOND)
    at_north = -face(own[3], others[3], SECOND)
    for copy in reads:
        copy.wait()
    for held, row, term in ((top, 0, at_west), (bottom, rows - 1, at_east)):
        low[row] = low[row] + term[:8]
        held[...] = held[...] + term[8 : cols - 8]
        high[row] = high[row] + term[cols - 8 :]
    low[:, 0, :] = low[:, 0, :] + at_south
    high[:, 7, :] = high[:, 7, :] + at_north
    writes = [
        pltpu.make_async_copy(held, out.at[p], sems.at[k]) for k, (held, p) in enumerate(places)
    ]
    for copy in writes:
        copy.start()
    for copy in writes:
        copy.wait()


def in_vmem():
    return pl.BlockSpec(memory_space=pltpu.VMEM)


def in_smem():
    return pl.BlockSpec(memory_space=pltpu.SMEM)


def interior(air_state, tile_class, edge_map, weights):
    return pl.pallas_call(
        main_kernel,
        out_shape=[
            jax.ShapeDtypeStruct(air_state.shape, jnp.float32),
            jax.ShapeDtypeStruct((4,), jnp.int32),
        ],
        in_specs=[in_vmem(), in_smem(), in_smem()] + [in_vmem()] * len(weights),
        out_specs=[in_vmem(), in_smem()],
        compiler_params=pltpu.CompilerParams(vmem_limit_bytes=48 * 1024 * 1024),
        cost_estimate=pl.CostEstimate(
            flops=3_200_000_000, bytes_accessed=4_200_000, transcendentals=3_000_000
        ),
        name="columns_and_interior",
    )(air_state, tile_class, edge_map, *weights)


def boundary(codes, edges, traces, partial):
    rows, cols, feat = partial.shape
    return pl.pallas_call(
        edge_kernel,
        out_shape=jax.ShapeDtypeStruct(partial.shape, jnp.float32),
        in_specs=[in_smem()] + [in_vmem()] * 5 + [pl.BlockSpec(memory_space=pl.ANY)],
        out_specs=pl.BlockSpec(memory_space=pl.ANY),
        scratch_shapes=[
            pltpu.VMEM((rows, 8, feat), jnp.float32),
            pltpu.VMEM((rows, 8, feat), jnp.float32),
            pltpu.VMEM((cols - 16, feat), jnp.float32),
            pltpu.VMEM((cols - 16, feat), jnp.float32),
            pltpu.SemaphoreType.DMA((4,)),
        ],
        input_output_aliases={6: 0},
        compiler_params=pltpu.CompilerParams(vmem_limit_bytes=8 * 1024 * 1024),
        cost_estimate=pl.CostEstimate(flops=2_000_000, bytes_accessed=600_000, transcendentals=0),
        name="boundary_faces",
    )(codes, edges, *traces, partial)


def shifted(x, axis, step):
    peers = lax.axis_size(axis)
    return lax.ppermute(x, axis, [(i, (i + step) % peers) for i in range(peers)])


def on_device(
    air_state,
    edge_map,
    tile_class,
    in_weight,
    in_bias,
    mid_weight,
    mid_bias,
    out_weight,
    land_in,
    land_bias,
    land_out,
):
    edges = jnp.stack([air_state[0], air_state[-1], air_state[:, 0], air_state[:, -1]])
    traces = [
        shifted(edges, "gx", 1),
        shifted(edges, "gx", -1),
        shifted(edges, "gy", 1),
        shifted(edges, "gy", -1),
    ]
    weights = (
        in_weight,
        in_bias.reshape(1, -1),
        mid_weight,
        mid_bias.reshape(1, -1),
        out_weight,
        land_in,
        land_bias.reshape(1, -1),
        land_out,
    )
    partial, codes = interior(air_state, tile_class, edge_map.transpose(0, 2, 1), weights)
    return boundary(codes, edges, traces, partial)


def solution(mesh):
    row_split, col_split = P("gx", "gy", None), P(None, "gy", None)
    return jax.shard_map(
        on_device,
        mesh=mesh,
        in_specs=(row_split, P(), col_split) + (P(),) * 8,
        out_specs=row_split,
        check_vma=False,
    )
```

```python
import functools
import math

import jax
import jax.numpy as jnp
import numpy as np
from jax import lax
from jax.experimental import pallas as pl
from jax.experimental.pallas import tpu as pltpu
from jax.sharding import PartitionSpec as P

CHUNK = 16
TILE = 64
GROUP = 8
WRAP = 8
FIRST, SECOND = "first", "second"


def lobatto_derivative():
    points = np.array([-1.0, -math.sqrt(0.2), math.sqrt(0.2), 1.0])
    barycentric = np.array(
        [1.0 / np.prod([points[j] - points[k] for k in range(4) if k != j]) for j in range(4)]
    )
    derivative = np.zeros((4, 4))
    for i in range(4):
        for j in range(4):
            if i != j:
                derivative[i, j] = barycentric[j] / barycentric[i] / (points[i] - points[j])
        derivative[i, i] = -np.sum([derivative[i, k] for k in range(4) if k != i])
    return derivative


def lane_block(shape):
    return lax.broadcasted_iota(jnp.int32, shape, len(shape) - 1) // 32


def spread(values, block, source):
    axis = values.ndim - 1
    if source == 0:
        once = jnp.where(block == 0, values, pltpu.roll(values, 32, axis))
        return jnp.where(block < 2, once, pltpu.roll(once, 64, axis))
    if source == 1:
        once = jnp.where(block == 1, values, pltpu.roll(values, 96, axis))
        return jnp.where(block < 2, once, pltpu.roll(once, 64, axis))
    once = jnp.where(block == 2, values, pltpu.roll(values, 32, axis))
    return jnp.where(block >= 2, once, pltpu.roll(once, 64, axis))


def primitives(states):
    flat = states.reshape(-1, states.shape[-1])
    block = lane_block(flat.shape)
    density = spread(flat, block, 0)
    carried = flat / density
    first = spread(carried, block, 1)
    second = spread(carried, block, 2)
    carried = jnp.where(block == 0, 1.0, carried)
    half_pressure = 0.25 * flat
    zero = jnp.zeros_like(flat)
    pressure_first = jnp.where(block == 1, pltpu.roll(half_pressure, 64, 1), zero)
    pressure_second = jnp.where(block == 2, pltpu.roll(half_pressure, 96, 1), zero)
    back = lambda x: x.reshape(states.shape)
    return {
        "q": states,
        "d": back(density),
        "c": back(carried),
        FIRST: (back(0.125 * first), back(pressure_first)),
        SECOND: (back(0.125 * second), back(pressure_second)),
    }


def pick(prims, index):
    out = {k: prims[k][index] for k in ("q", "d", "c")}
    for k in (FIRST, SECOND):
        out[k] = tuple(x[index] for x in prims[k])
    return out


def flux(one, two, axis):
    return (one["d"] + two["d"]) * (one[axis][0] + two[axis][0]) * (one["c"] + two["c"]) + (
        one[axis][1] + two[axis][1]
    )


def face(left, right, axis):
    wave = 8.0 * jnp.maximum(jnp.abs(left[axis][0]), jnp.abs(right[axis][0])) + 1.0
    return 6.0 * flux(left, right, axis) - (3.0 * wave) * (right["q"] - left["q"])


def volume(nodes, axis):
    derivative = lobatto_derivative()
    fluxes = {}
    for a in range(4):
        for b in range(a + 1, 4):
            fluxes[a, b] = fluxes[b, a] = flux(nodes[a], nodes[b], axis)
    results = []
    for a in range(4):
        total = None
        for b in range(4):
            if b != a:
                term = (-2.0 * float(derivative[a, b])) * fluxes[a, b]
                total = term if total is None else total + term
        results.append(total)
    return results


def silu(z):
    half = 0.5 * z
    return (half + half * jnp.tanh(half)).astype(jnp.bfloat16)


def dot(a, b):
    return jnp.dot(a, b, preferred_element_type=jnp.float32)


def ahead(row, col):
    return (row % WRAP == 0) & ((row > 0) | (col > 0))


def turned(edge):
    count = edge.shape[0] // 8
    place = lax.broadcasted_iota(jnp.int32, (8, edge.shape[1]), 0)
    pieces = []
    for k in range(count):
        piece = edge[(count - 1 - k) * 8 : (count - k) * 8]
        piece = pltpu.roll(piece, 4, 0)
        piece = jnp.where(place % 4 < 2, pltpu.roll(piece, 6, 0), pltpu.roll(piece, 2, 0))
        piece = jnp.where(place % 2 < 1, pltpu.roll(piece, 7, 0), pltpu.roll(piece, 1, 0))
        pieces.append(piece)
    return jnp.concatenate(pieces, axis=0)


def pack_kernel(n_x, n_y, air, edge_map, own, wrap, row_even, row_odd, col_even, col_odd, back, maps, sems):
    rows, cols, _ = air.shape
    row, col = lax.axis_index("gx"), lax.axis_index("gy")
    west, east = (row + n_x - 1) % n_x, (row + 1) % n_x
    south, north = (col + n_y - 1) % n_y, (col + 1) % n_y
    copies = [
        pltpu.make_async_copy(air.at[:, 0], own.at[2], sems.at[0]),
        pltpu.make_async_copy(air.at[:, cols - 1], own.at[3], sems.at[1]),
        pltpu.make_async_copy(air.at[0], own.at[0], sems.at[2]),
        pltpu.make_async_copy(air.at[rows - 1], own.at[1], sems.at[3]),
        pltpu.make_async_copy(edge_map.at[west], maps.at[0], sems.at[4]),
        pltpu.make_async_copy(edge_map.at[row], maps.at[1], sems.at[5]),
        pltpu.make_async_copy(edge_map.at[east], maps.at[2], sems.at[6]),
    ]
    for copy in copies:
        copy.start()
    for copy in copies:
        copy.wait()

    def asked(code):
        edge = own[code % 4]
        return jnp.where(code >= 4, turned(edge), edge)

    to_west = asked(maps[0, 1, col])
    to_east = asked(maps[2, 0, col])
    to_south = asked(maps[1, 3, south])
    to_north = asked(maps[1, 2, north])
    even = row % 2 == 0
    row_even[...] = jnp.where(even, to_east, to_west)
    odd = jnp.where(even, to_west, to_east)
    row_odd[...] = odd
    wrap[...] = odd
    back[...] = odd
    even = col % 2 == 0
    col_even[...] = jnp.where(even, to_north, to_south)
    col_odd[...] = jnp.where(even, to_south, to_north)


def main_kernel(early, inputs, moved, result, scratch):
    held, sems, move_sems, normed, base, listed, fields, total = scratch
    row = lax.axis_index("gx")
    col = lax.axis_index("gy")
    moves = start_moves(moved, move_sems, row)

    @pl.when(ahead(row, col) == early)
    def _():
        copies = []
        for k, (source, target) in enumerate(zip(inputs, held)):
            if k == 1:
                source = source.at[row]
            copies.append(pltpu.make_async_copy(source, target, sems.at[k]))
        for k in (0, 2, 3, 6, 1, 7, 8, 4, 5, 9):
            copies[k].start()

        def ready(*numbers):
            for k in numbers:
                copies[k].wait()

        columns_and_interior(held, ready, normed, base, listed, fields, total)
        end = pltpu.make_async_copy(total, result, sems.at[0])
        end.start()
        end.wait()

    end_moves(moves, row)


def start_moves(moved, sems, row):
    moves = []
    for sources, target, wanted in moved:
        first = sum(len(copies) for copies, _ in moves)
        copies = [
            pltpu.make_async_copy(ref, target.at[k], sems.at[first + k])
            for k, ref in enumerate(sources)
        ]
        moves.append((copies, wanted))
    for copies, wanted in moves:

        @pl.when(wanted(row))
        def _():
            for copy in copies:
                copy.start()

    return moves


def end_moves(moves, row):
    for copies, wanted in moves:

        @pl.when(wanted(row))
        def _():
            for copy in copies:
                copy.wait()


def two_layers(x, weight, bias, last):
    return dot(silu(dot(x, weight[...]) + bias[...]), last[...])


def columns_and_interior(held, ready, normed_ref, base, listed, fields, out):
    air, classes, in_w, in_b, mid_w, mid_b, out_w, land_in, land_b, land_out = held
    rows, cols, feat = air.shape
    tiles = rows * cols // TILE
    chunk_cols = CHUNK * cols

    ready(0, 2, 3, 6)

    def base_chunk(c, carry):
        start = pl.multiple_of(c * CHUNK, CHUNK)
        columns = air[pl.ds(start, CHUNK)].reshape(chunk_cols, feat).astype(jnp.bfloat16)
        values = columns.astype(jnp.float32)
        mean = jnp.sum(values * values, axis=-1, keepdims=True) * (1.0 / feat)
        normed = (values * lax.rsqrt(mean + 1e-06)).astype(jnp.bfloat16)
        place = pl.ds(pl.multiple_of(c * chunk_cols, chunk_cols), chunk_cols)
        normed_ref[place, :] = normed
        base[place, :] = two_layers(normed, in_w, in_b, out_w)
        store_fields(start, CHUNK, air, fields)
        return carry

    lax.fori_loop(0, rows // CHUNK, base_chunk, 0)

    ready(1)

    def note(t, count):
        listed[count] = t
        return count + classes[0, t]

    lands = lax.fori_loop(0, tiles, note, 0)
    for k in range(GROUP):
        listed[lands + k] = tiles

    @pl.when(lands > 0)
    def _():
        ready(4, 5, 7, 8, 9)

    def land_group(g, carry):
        numbers = [listed[g * GROUP + k] for k in range(GROUP)]
        starts = [pl.multiple_of(t * TILE, TILE) for t in numbers]
        normed = jnp.concatenate([normed_ref[pl.ds(s, TILE), :] for s in starts], axis=0)
        land = silu(dot(normed, land_in[...]) + land_b[...])
        term = two_layers(land, mid_w, mid_b, land_out)
        for k, s in enumerate(starts):
            base[pl.ds(s, TILE), :] = base[pl.ds(s, TILE), :] + term[k * TILE : (k + 1) * TILE]
        return carry

    lax.fori_loop(0, (lands + GROUP - 1) // GROUP, land_group, 0)
    interior_and_sum(air, fields, base, out)

    @pl.when(lands == 0)
    def _():
        ready(4, 5, 7, 8, 9)


def store_fields(start, count, air, fields):
    _, cols, feat = air.shape
    elements = cols // 4
    for a in range(4):
        states = air[pl.ds(start, count), pl.ds(a, elements, stride=4), :]
        flat = states.reshape(-1, feat)
        block = lane_block(flat.shape)
        density = spread(flat, block, 0)
        carried = flat * pl.reciprocal(density)
        speeds = 0.125 * carried
        half_pressure = 0.25 * flat
        values = (
            density,
            jnp.where(block == 0, 1.0, carried),
            spread(speeds, block, 1),
            spread(speeds, block, 2),
            jnp.where(block == 1, pltpu.roll(half_pressure, 64, 1), 0.0),
            jnp.where(block == 2, pltpu.roll(half_pressure, 96, 1), 0.0),
        )
        for k, value in enumerate(values):
            fields[k, pl.ds(start, count), a] = value.reshape(states.shape)


def node_fields(fields, row, a):
    d, c, u, v, p, s = (fields[k, row, a] for k in range(6))
    return {"d": d, "c": c, "q": d * c, FIRST: (u, p), SECOND: (v, s)}


def interior_and_sum(air, fields, base, out):
    rows, cols, feat = air.shape
    elements = cols // 4
    count = rows // 4
    number = lax.broadcasted_iota(jnp.int32, (elements, feat), 0)

    def element(e, below):
        start = e * 4
        after = jnp.minimum(start + 4, rows - 1)
        inside = jnp.where(e < count - 1, 1.0, 0.0)
        sums = [[None] * 4 for _ in range(4)]
        above = []
        for a in range(4):
            nodes = [node_fields(fields, start + r, a) for r in range(4)]
            totals = volume(nodes, FIRST)
            high = inside * face(nodes[3], node_fields(fields, after, a), FIRST)
            above.append(high)
            totals[0] = totals[0] + below[a]
            totals[3] = totals[3] - high
            for r in range(4):
                sums[r][a] = totals[r]
        for r in range(4):
            nodes = [node_fields(fields, start + r, a) for a in range(4)]
            totals = volume(nodes, SECOND)
            lower = jax.tree.map(lambda x: pltpu.roll(x, 1, 0), nodes[3])
            faces = jnp.where(number == 0, 0.0, face(lower, nodes[0], SECOND))
            totals[0] = totals[0] + faces
            totals[3] = totals[3] - pltpu.roll(faces, elements - 1, 0)
            for a in range(4):
                along = pl.ds(a, elements, stride=4)
                out[start + r, along, :] = sums[r][a] + totals[a]
        physics = base[pl.ds(pl.multiple_of(start * cols, 4 * cols), 4 * cols), :]
        physics = physics.astype(jnp.bfloat16).astype(jnp.float32).reshape(4, cols, feat)
        out[pl.ds(start, 4)] = out[pl.ds(start, 4)] + physics
        return tuple(above)

    zero = jnp.zeros((elements, feat), jnp.float32)
    lax.fori_loop(0, count, element, (zero,) * 4)


def edge_kernel(edges, early, late, from_low, from_high, partial, out, low, high, top, bottom, sems):
    col_even_a, col_odd_a, row_odd_a, row_even_a = (early[k] for k in range(4))
    col_even_b, col_odd_b, row_even_b = (late[k] for k in range(3))
    rows, cols, feat = out.shape
    first, middle, final = pl.ds(0, 8), pl.ds(8, cols - 16), pl.ds(cols - 8, 8)
    inner = (pl.ds(1, rows - 2), middle)
    inside = pltpu.make_async_copy(partial.at[inner], out.at[inner], sems.at[4])
    inside.start()
    row, col = lax.axis_index("gx"), lax.axis_index("gy")
    place = row % WRAP
    last_row = place == WRAP - 1
    first_x = jnp.where(place < WRAP - 2, row_even_a, row_even_b)
    wrapped = jnp.where(place == 0, from_low[...], from_high[...])
    second_x = jnp.where((place == 0) | last_row, wrapped, row_odd_a)
    even = row % 2 == 0
    west = jnp.where(even, second_x, first_x)
    east = jnp.where(even, first_x, second_x)
    first_y = jnp.where(last_row, col_even_b, col_even_a)
    second_y = jnp.where(last_row, col_odd_b, col_odd_a)
    even = col % 2 == 0
    south = jnp.where(even, second_y, first_y)
    north = jnp.where(even, first_y, second_y)
    own = [primitives(edges[s]) for s in range(4)]
    west, east, south, north = (primitives(x) for x in (west, east, south, north))
    at_west = face(west, own[0], FIRST)
    at_east = -face(own[1], east, FIRST)
    at_south = face(south, own[2], SECOND)
    at_north = -face(own[3], north, SECOND)
    low[...] = partial[:, :8]
    high[...] = partial[:, cols - 8 :]
    for held, r, term in ((top, 0, at_west), (bottom, rows - 1, at_east)):
        low[r] = low[r] + term[:8]
        held[...] = partial[r, 8 : cols - 8] + term[8 : cols - 8]
        high[r] = high[r] + term[cols - 8 :]
    low[:, 0, :] = low[:, 0, :] + at_south
    high[:, 7, :] = high[:, 7, :] + at_north
    places = [
        (low, (slice(None), first)),
        (high, (slice(None), final)),
        (top, (0, middle)),
        (bottom, (rows - 1, middle)),
    ]
    writes = [
        pltpu.make_async_copy(held, out.at[p], sems.at[k]) for k, (held, p) in enumerate(places)
    ]
    for copy in writes:
        copy.start()
    for copy in writes:
        copy.wait()
    inside.wait()


def in_vmem():
    return pl.BlockSpec(memory_space=pltpu.VMEM)


def in_hbm():
    return pl.BlockSpec(memory_space=pltpu.HBM)


def anywhere():
    return pl.BlockSpec(memory_space=pl.ANY)


def kept_in_hbm(x):
    return pltpu.with_memory_space_constraint(x, pltpu.HBM)


def vmem_array(shape, dtype):
    return pltpu.VMEM(shape, dtype)


def kept_in_vmem(x):
    return pltpu.with_memory_space_constraint(x, pltpu.VMEM)


def packed(air_state, edge_map, n_x, n_y):
    rows, cols, feat = air_state.shape
    return pl.pallas_call(
        functools.partial(pack_kernel, n_x, n_y),
        out_shape=[vmem_array((4, cols, feat), jnp.float32)]
        + [vmem_array((cols, feat), jnp.float32)] * 6,
        in_specs=[in_hbm()] * 2,
        out_specs=[in_vmem()] * 7,
        scratch_shapes=[
            pltpu.SMEM((3,) + edge_map.shape[1:], jnp.int32),
            pltpu.SemaphoreType.DMA((7,)),
        ],
        compiler_params=pltpu.CompilerParams(vmem_limit_bytes=4 * 1024 * 1024),
        name="own_edges",
    )(kept_in_hbm(air_state), kept_in_hbm(edge_map))


def idle_kernel(*refs):
    pass


def nothing(count):
    def make(*edges):
        x = edges[0]
        return tuple(
            pl.pallas_call(
                idle_kernel,
                out_shape=[jax.ShapeDtypeStruct(x.shape, x.dtype)] * count,
                in_specs=[anywhere()],
                out_specs=[anywhere()] * count,
                name="no_exchange",
            )(x)
        )

    return make


def interior(early, inputs, passed, started=(), groups=()):
    air_state = inputs[0]
    held = []
    for k, x in enumerate(inputs):
        space = pltpu.SMEM if k == 1 else pltpu.VMEM
        held.append(space(x.shape[1:] if k == 1 else x.shape, x.dtype))
    like = lambda x: vmem_array(x.shape, x.dtype)
    outs = [vmem_array(air_state.shape, jnp.float32)]
    outs += [like(x) for x in started[1:]]
    n_in, n_passed, n_started = len(inputs), len(passed), len(started)
    targets = []
    for arrays, _, number in groups:
        targets.append(len(outs) if number is None else number)
        if number is None:
            outs.append(vmem_array((len(arrays),) + arrays[0].shape, arrays[0].dtype))
    every = [x for arrays, _, _ in groups for x in arrays]
    n_fixed = len(outs)
    aliases = {n_in + k: n_fixed + k for k in range(n_passed)}
    aliases.update({n_in + n_passed + k: k for k in range(n_started)})
    rows, cols, feat = air_state.shape
    tiles = rows * cols // TILE

    def kernel(*refs):
        refs = list(refs)
        n_before = n_in + n_passed + n_started
        results = refs[n_before + len(every) :][: n_fixed + n_passed]
        rest = refs[n_before + len(every) + len(results) :]
        moved, at = [], n_before
        for (arrays, wanted, _), target in zip(groups, targets):
            moved.append((refs[at : at + len(arrays)], results[target], wanted))
            at += len(arrays)
        main_kernel(early, refs[:n_in], moved, results[0], (rest[:n_in], *rest[n_in:]))

    return pl.pallas_call(
        kernel,
        out_shape=outs + [like(x) for x in passed],
        in_specs=[in_hbm()] * n_in
        + [in_vmem()] * (n_passed + n_started)
        + [anywhere()] * len(every),
        out_specs=[in_vmem()] * (n_fixed + n_passed),
        scratch_shapes=held
        + [
            pltpu.SemaphoreType.DMA((n_in,)),
            pltpu.SemaphoreType.DMA((max(len(every), 1),)),
            pltpu.VMEM((rows * cols + TILE, feat), jnp.bfloat16),
            pltpu.VMEM((rows * cols + TILE, feat), jnp.float32),
            pltpu.SMEM((tiles + GROUP,), jnp.int32),
            pltpu.VMEM((6, rows, 4, cols // 4, feat), jnp.float32),
            pltpu.VMEM(air_state.shape, jnp.float32),
        ],
        input_output_aliases=aliases,
        compiler_params=pltpu.CompilerParams(vmem_limit_bytes=32 * 1024 * 1024),
        cost_estimate=pl.CostEstimate(
            flops=1_000_000_000, bytes_accessed=4_200_000, transcendentals=1_000_000
        ),
        name="columns_ahead" if early else "columns_behind",
    )(*map(kept_in_hbm, inputs), *map(kept_in_vmem, (*passed, *started)), *every)


def collected(arrays, wanted, passed):
    count, n_passed = len(arrays), len(passed)
    like = lambda x: vmem_array(x.shape, x.dtype)

    def kernel(*refs):
        row = lax.axis_index("gx")
        sources, target, sems = refs[:count], refs[count + n_passed], refs[-1]
        end_moves(start_moves([(sources, target, wanted)], sems, row), row)

    return pl.pallas_call(
        kernel,
        out_shape=[vmem_array((count,) + arrays[0].shape, arrays[0].dtype)]
        + [like(x) for x in passed],
        in_specs=[anywhere()] * count + [in_vmem()] * n_passed,
        out_specs=[in_vmem()] * (1 + n_passed),
        scratch_shapes=[pltpu.SemaphoreType.DMA((count,))],
        input_output_aliases={count + k: 1 + k for k in range(n_passed)},
        name="early_traces",
    )(*arrays, *map(kept_in_vmem, passed))


def boundary(edges, early, late, from_low, from_high, partial):
    rows, cols, feat = partial.shape
    return pl.pallas_call(
        edge_kernel,
        out_shape=jax.ShapeDtypeStruct(partial.shape, jnp.float32),
        in_specs=[in_vmem()] * 6,
        out_specs=in_hbm(),
        scratch_shapes=[
            pltpu.VMEM((rows, 8, feat), jnp.float32),
            pltpu.VMEM((rows, 8, feat), jnp.float32),
            pltpu.VMEM((cols - 16, feat), jnp.float32),
            pltpu.VMEM((cols - 16, feat), jnp.float32),
            pltpu.SemaphoreType.DMA((5,)),
        ],
        compiler_params=pltpu.CompilerParams(vmem_limit_bytes=8 * 1024 * 1024),
        cost_estimate=pl.CostEstimate(flops=2_000_000, bytes_accessed=600_000, transcendentals=0),
        name="boundary_faces",
    )(edges, early, late, from_low, from_high, partial)


def swap(rows, cols, n_y):
    pairs = []
    for r, other_r in rows:
        for c, other_c in cols:
            one, two = r * n_y + c, other_r * n_y + other_c
            pairs += [(one, two), (two, one)]
    return pairs


def on_device(
    air_state,
    edge_map,
    tile_class,
    in_weight,
    in_bias,
    mid_weight,
    mid_bias,
    out_weight,
    land_in,
    land_bias,
    land_out,
):
    n_x, n_y = lax.axis_size("gx"), lax.axis_size("gy")
    inputs = (
        air_state,
        tile_class,
        in_weight,
        in_bias.reshape(1, -1),
        mid_weight,
        mid_bias.reshape(1, -1),
        out_weight,
        land_in,
        land_bias.reshape(1, -1),
        land_out,
    )
    row = lax.axis_index("gx")
    late = [i for i in range(n_x) if i % WRAP == WRAP - 1]
    early = [i for i in range(n_x) if i not in late]
    evens = [(i, i + 1) for i in range(0, n_x, 2)]
    odds = [(i, (i + 1) % n_x) for i in range(1, n_x, 2)]
    col_evens = [(j, j + 1) for j in range(0, n_y, 2)]
    col_odds = [(j, (j + 1) % n_y) for j in range(1, n_y, 2)]
    col_same = [(j, j) for j in range(n_y)]

    def move(x, rows, cols):
        return lax.ppermute(x, ("gx", "gy"), swap(rows, cols, n_y))

    def exchange_early(row_even, row_odd, col_odd, col_even):
        same = [(i, i) for i in early]
        return (
            move(col_even, same, col_evens),
            move(col_odd, same, col_odds),
            move(row_odd, [p for p in odds if p[0] not in late], col_same),
            move(row_even, [p for p in evens if p[1] not in late], col_same),
        )

    def exchange_late(row_even, col_odd, col_even):
        same = [(i, i) for i in late]
        return (
            move(col_even, same, col_evens),
            move(col_odd, same, col_odds),
            move(row_even, [p for p in evens if p[1] in late], col_same),
        )

    def across(x, rows):
        return lax.ppermute(
            x, ("gx", "gy"), [(a * n_y + j, b * n_y + j) for a, b in rows for j in range(n_y)]
        )

    place = row % WRAP
    wraps = [p for p in odds if p[0] in late]
    is_first = lambda r: r % WRAP == 0
    is_middle = lambda r: (r % WRAP > 0) & (r % WRAP < WRAP - 1)
    is_late = lambda r: r % WRAP >= WRAP - 2
    own, wrap, row_even, row_odd, col_even, col_odd, back = packed(
        air_state, edge_map.transpose(0, 2, 1), n_x, n_y
    )
    partial, wrap, row_even, row_odd, col_even, col_odd, back = interior(
        True, inputs, (wrap, row_even, row_odd, col_even, col_odd, back)
    )
    from_low = across(wrap, wraps)
    early_traces = lax.cond(
        place < WRAP - 1, exchange_early, nothing(4), row_even, row_odd, col_odd, col_even
    )
    early_held, back = collected(early_traces, is_first, (back,))
    from_high = across(back, [(b, a) for a, b in wraps])
    late_traces = lax.cond(
        place >= WRAP - 2, exchange_late, nothing(3), row_even, col_odd, col_even
    )
    partial, early_held, late_held = interior(
        False,
        inputs,
        (),
        (partial, early_held),
        ((early_traces, is_middle, 1), (late_traces, is_late, None)),
    )
    return boundary(own, early_held, late_held, from_low, from_high, partial)


def solution(mesh):
    row_split, col_split = P("gx", "gy", None), P(None, "gy", None)
    return jax.shard_map(
        on_device,
        mesh=mesh,
        in_specs=(row_split, P(), col_split) + (P(),) * 8,
        out_specs=row_split,
        check_vma=False,
    )
```

```python
import functools
import math

import jax
import jax.numpy as jnp
import numpy as np
from jax import lax
from jax.experimental import pallas as pl
from jax.experimental.pallas import tpu as pltpu
from jax.sharding import PartitionSpec as P

CHUNK = 16
TILE = 64
GROUP = 8
WRAP = 8
FIRST, SECOND = "first", "second"


def lobatto_derivative():
    points = np.array([-1.0, -math.sqrt(0.2), math.sqrt(0.2), 1.0])
    barycentric = np.array(
        [1.0 / np.prod([points[j] - points[k] for k in range(4) if k != j]) for j in range(4)]
    )
    derivative = np.zeros((4, 4))
    for i in range(4):
        for j in range(4):
            if i != j:
                derivative[i, j] = barycentric[j] / barycentric[i] / (points[i] - points[j])
        derivative[i, i] = -np.sum([derivative[i, k] for k in range(4) if k != i])
    return derivative


def lane_block(shape):
    return lax.broadcasted_iota(jnp.int32, shape, len(shape) - 1) // 32


def spread(values, block, source):
    axis = values.ndim - 1
    if source == 0:
        once = jnp.where(block == 0, values, pltpu.roll(values, 32, axis))
        return jnp.where(block < 2, once, pltpu.roll(once, 64, axis))
    if source == 1:
        once = jnp.where(block == 1, values, pltpu.roll(values, 96, axis))
        return jnp.where(block < 2, once, pltpu.roll(once, 64, axis))
    once = jnp.where(block == 2, values, pltpu.roll(values, 32, axis))
    return jnp.where(block >= 2, once, pltpu.roll(once, 64, axis))


def primitives(states):
    flat = states.reshape(-1, states.shape[-1])
    block = lane_block(flat.shape)
    density = spread(flat, block, 0)
    carried = flat / density
    first = spread(carried, block, 1)
    second = spread(carried, block, 2)
    carried = jnp.where(block == 0, 1.0, carried)
    half_pressure = 0.25 * flat
    zero = jnp.zeros_like(flat)
    pressure_first = jnp.where(block == 1, pltpu.roll(half_pressure, 64, 1), zero)
    pressure_second = jnp.where(block == 2, pltpu.roll(half_pressure, 96, 1), zero)
    back = lambda x: x.reshape(states.shape)
    return {
        "q": states,
        "d": back(density),
        "c": back(carried),
        FIRST: (back(0.125 * first), back(pressure_first)),
        SECOND: (back(0.125 * second), back(pressure_second)),
    }


def pick(prims, index):
    out = {k: prims[k][index] for k in ("q", "d", "c")}
    for k in (FIRST, SECOND):
        out[k] = tuple(x[index] for x in prims[k])
    return out


def flux(one, two, axis):
    return (one["d"] + two["d"]) * (one[axis][0] + two[axis][0]) * (one["c"] + two["c"]) + (
        one[axis][1] + two[axis][1]
    )


def face(left, right, axis):
    wave = 8.0 * jnp.maximum(jnp.abs(left[axis][0]), jnp.abs(right[axis][0])) + 1.0
    return 6.0 * flux(left, right, axis) - (3.0 * wave) * (right["q"] - left["q"])


def volume(nodes, axis):
    derivative = lobatto_derivative()
    fluxes = {}
    for a in range(4):
        for b in range(a + 1, 4):
            fluxes[a, b] = fluxes[b, a] = flux(nodes[a], nodes[b], axis)
    results = []
    for a in range(4):
        total = None
        for b in range(4):
            if b != a:
                term = (-2.0 * float(derivative[a, b])) * fluxes[a, b]
                total = term if total is None else total + term
        results.append(total)
    return results


def silu(z):
    half = 0.5 * z
    return (half + half * jnp.tanh(half)).astype(jnp.bfloat16)


def dot(a, b):
    return jnp.dot(a, b, preferred_element_type=jnp.float32)


def ahead(row, col):
    return ((row % WRAP == 0) & ((row > 0) | (col > 0))) | ((row == 1) & (col == 0))


def turned(edge):
    count = edge.shape[0] // 8
    place = lax.broadcasted_iota(jnp.int32, (8, edge.shape[1]), 0)
    pieces = []
    for k in range(count):
        piece = edge[(count - 1 - k) * 8 : (count - k) * 8]
        piece = pltpu.roll(piece, 4, 0)
        piece = jnp.where(place % 4 < 2, pltpu.roll(piece, 6, 0), pltpu.roll(piece, 2, 0))
        piece = jnp.where(place % 2 < 1, pltpu.roll(piece, 7, 0), pltpu.roll(piece, 1, 0))
        pieces.append(piece)
    return jnp.concatenate(pieces, axis=0)


def pack_kernel(n_x, n_y, air, edge_map, own, late_even, wrap, row_even, row_odd, col_even, col_odd, back, maps, sems):
    rows, cols, _ = air.shape
    row, col = lax.axis_index("gx"), lax.axis_index("gy")
    west, east = (row + n_x - 1) % n_x, (row + 1) % n_x
    south, north = (col + n_y - 1) % n_y, (col + 1) % n_y
    copies = [
        pltpu.make_async_copy(air.at[:, 0], own.at[2], sems.at[0]),
        pltpu.make_async_copy(air.at[:, cols - 1], own.at[3], sems.at[1]),
        pltpu.make_async_copy(air.at[0], own.at[0], sems.at[2]),
        pltpu.make_async_copy(air.at[rows - 1], own.at[1], sems.at[3]),
        pltpu.make_async_copy(edge_map.at[west], maps.at[0], sems.at[4]),
        pltpu.make_async_copy(edge_map.at[row], maps.at[1], sems.at[5]),
        pltpu.make_async_copy(edge_map.at[east], maps.at[2], sems.at[6]),
    ]
    for copy in copies:
        copy.start()
    for copy in copies:
        copy.wait()

    def asked(code):
        edge = own[code % 4]
        return jnp.where(code >= 4, turned(edge), edge)

    to_west = asked(maps[0, 1, col])
    to_east = asked(maps[2, 0, col])
    to_south = asked(maps[1, 3, south])
    to_north = asked(maps[1, 2, north])
    even = row % 2 == 0
    row_even[...] = jnp.where(even, to_east, to_west)
    odd = jnp.where(even, to_west, to_east)
    late_even[...] = row_even[...]
    row_odd[...] = odd
    wrap[...] = odd
    back[...] = odd
    even = col % 2 == 0
    col_even[...] = jnp.where(even, to_north, to_south)
    col_odd[...] = jnp.where(even, to_south, to_north)


def main_kernel(early, inputs, moved, result, scratch):
    held, sems, move_sems, normed, base, listed, fields = scratch
    row = lax.axis_index("gx")
    col = lax.axis_index("gy")
    moves = start_moves(moved, move_sems, row)

    @pl.when(ahead(row, col) == early)
    def _():
        copies = []
        for k, (source, target) in enumerate(zip(inputs, held)):
            if k == 1:
                source = source.at[row]
            copies.append(pltpu.make_async_copy(source, target, sems.at[k]))
        for k in (0, 2, 3, 6, 1, 7, 8, 4, 5, 9):
            copies[k].start()

        def ready(*numbers):
            for k in numbers:
                copies[k].wait()

        columns_and_interior(held, ready, normed, base, listed, fields, result)

    end_moves(moves, row)


def start_moves(moved, sems, row):
    moves = []
    for sources, target, wanted in moved:
        first = sum(len(copies) for copies, _ in moves)
        copies = [
            pltpu.make_async_copy(ref, target.at[k], sems.at[first + k])
            for k, ref in enumerate(sources)
        ]
        moves.append((copies, wanted))
    for copies, wanted in moves:

        @pl.when(wanted(row))
        def _():
            for copy in copies:
                copy.start()

    return moves


def end_moves(moves, row):
    for copies, wanted in moves:

        @pl.when(wanted(row))
        def _():
            for copy in copies:
                copy.wait()


def two_layers(x, weight, bias, last):
    return dot(silu(dot(x, weight[...]) + bias[...]), last[...])


def columns_and_interior(held, ready, normed_ref, base, listed, fields, out):
    air, classes, in_w, in_b, mid_w, mid_b, out_w, land_in, land_b, land_out = held
    rows, cols, feat = air.shape
    tiles = rows * cols // TILE
    chunk_cols = CHUNK * cols

    ready(0, 2, 3, 6)

    def base_chunk(c, carry):
        start = pl.multiple_of(c * CHUNK, CHUNK)
        columns = air[pl.ds(start, CHUNK)].reshape(chunk_cols, feat).astype(jnp.bfloat16)
        values = columns.astype(jnp.float32)
        mean = jnp.sum(values * values, axis=-1, keepdims=True) * (1.0 / feat)
        normed = (values * lax.rsqrt(mean + 1e-06)).astype(jnp.bfloat16)
        place = pl.ds(pl.multiple_of(c * chunk_cols, chunk_cols), chunk_cols)
        normed_ref[place, :] = normed
        base[place, :] = two_layers(normed, in_w, in_b, out_w)
        store_fields(start, CHUNK, air, fields)
        return carry

    lax.fori_loop(0, rows // CHUNK, base_chunk, 0)

    ready(1)

    def note(t, count):
        listed[count] = t
        return count + classes[0, t]

    lands = lax.fori_loop(0, tiles, note, 0)
    for k in range(GROUP):
        listed[lands + k] = tiles

    @pl.when(lands > 0)
    def _():
        ready(4, 5, 7, 8, 9)

    def land_group(first, count):
        starts = [pl.multiple_of(listed[first + k] * TILE, TILE) for k in range(count)]
        normed = jnp.concatenate([normed_ref[pl.ds(s, TILE), :] for s in starts], axis=0)
        land = silu(dot(normed, land_in[...]) + land_b[...])
        term = two_layers(land, mid_w, mid_b, land_out)
        for k, s in enumerate(starts):
            base[pl.ds(s, TILE), :] = base[pl.ds(s, TILE), :] + term[k * TILE : (k + 1) * TILE]

    def whole_group(g, carry):
        land_group(g * GROUP, GROUP)
        return carry

    half = GROUP // 2
    over = lands % GROUP
    whole = lands // GROUP + jnp.where(over > half, 1, 0)
    lax.fori_loop(0, whole, whole_group, 0)

    @pl.when((over > 0) & (over <= half))
    def _():
        land_group(whole * GROUP, half)

    interior_and_sum(air, fields, base, out)

    @pl.when(lands == 0)
    def _():
        ready(4, 5, 7, 8, 9)


def store_fields(start, count, air, fields):
    _, cols, feat = air.shape
    elements = cols // 4
    for a in range(4):
        states = air[pl.ds(start, count), pl.ds(a, elements, stride=4), :]
        flat = states.reshape(-1, feat)
        block = lane_block(flat.shape)
        density = spread(flat, block, 0)
        carried = flat * pl.reciprocal(density)
        speeds = 0.125 * carried
        half_pressure = 0.25 * flat
        values = (
            density,
            jnp.where(block == 0, 1.0, carried),
            spread(speeds, block, 1),
            spread(speeds, block, 2),
            jnp.where(block == 1, pltpu.roll(half_pressure, 64, 1), 0.0),
            jnp.where(block == 2, pltpu.roll(half_pressure, 96, 1), 0.0),
        )
        for k, value in enumerate(values):
            fields[k, pl.ds(start, count), a] = value.reshape(states.shape)


def node_fields(fields, row, a):
    d, c, u, v, p, s = (fields[k, row, a] for k in range(6))
    return {"d": d, "c": c, "q": d * c, FIRST: (u, p), SECOND: (v, s)}


def interior_and_sum(air, fields, base, out):
    rows, cols, feat = air.shape
    elements = cols // 4
    count = rows // 4
    number = lax.broadcasted_iota(jnp.int32, (elements, feat), 0)

    def element(e, below):
        start = e * 4
        after = jnp.minimum(start + 4, rows - 1)
        inside = jnp.where(e < count - 1, 1.0, 0.0)
        sums = [[None] * 4 for _ in range(4)]
        above = []
        for a in range(4):
            nodes = [node_fields(fields, start + r, a) for r in range(4)]
            totals = volume(nodes, FIRST)
            high = inside * face(nodes[3], node_fields(fields, after, a), FIRST)
            above.append(high)
            totals[0] = totals[0] + below[a]
            totals[3] = totals[3] - high
            for r in range(4):
                sums[r][a] = totals[r]
        for r in range(4):
            nodes = [node_fields(fields, start + r, a) for a in range(4)]
            totals = volume(nodes, SECOND)
            lower = jax.tree.map(lambda x: pltpu.roll(x, 1, 0), nodes[3])
            faces = jnp.where(number == 0, 0.0, face(lower, nodes[0], SECOND))
            totals[0] = totals[0] + faces
            totals[3] = totals[3] - pltpu.roll(faces, elements - 1, 0)
            for a in range(4):
                along = pl.ds(a, elements, stride=4)
                out[start + r, along, :] = sums[r][a] + totals[a]
        physics = base[pl.ds(pl.multiple_of(start * cols, 4 * cols), 4 * cols), :]
        physics = physics.astype(jnp.bfloat16).astype(jnp.float32).reshape(4, cols, feat)
        out[pl.ds(start, 4)] = out[pl.ds(start, 4)] + physics
        return tuple(above)

    zero = jnp.zeros((elements, feat), jnp.float32)
    lax.fori_loop(0, count, element, (zero,) * 4)


def edge_kernel(edges, early, late, from_low, from_high, partial, out, low, high, top, bottom, sems):
    col_even_a, col_odd_a, row_odd_a, row_even_a = (early[k] for k in range(4))
    col_even_b, col_odd_b, row_even_b = (late[k] for k in range(3))
    rows, cols, feat = out.shape
    first, middle, final = pl.ds(0, 8), pl.ds(8, cols - 16), pl.ds(cols - 8, 8)
    inner = (pl.ds(1, rows - 2), middle)
    inside = pltpu.make_async_copy(partial.at[inner], out.at[inner], sems.at[4])
    inside.start()
    row, col = lax.axis_index("gx"), lax.axis_index("gy")
    place = row % WRAP
    last_row = place == WRAP - 1
    first_x = jnp.where(place < WRAP - 2, row_even_a, row_even_b)
    wrapped = jnp.where(place == 0, from_low[...], from_high[...])
    second_x = jnp.where((place == 0) | last_row, wrapped, row_odd_a)
    even = row % 2 == 0
    west = jnp.where(even, second_x, first_x)
    east = jnp.where(even, first_x, second_x)
    first_y = jnp.where(last_row, col_even_b, col_even_a)
    second_y = jnp.where(last_row, col_odd_b, col_odd_a)
    even = col % 2 == 0
    south = jnp.where(even, second_y, first_y)
    north = jnp.where(even, first_y, second_y)
    own = [primitives(edges[s]) for s in range(4)]
    west, east, south, north = (primitives(x) for x in (west, east, south, north))
    at_west = face(west, own[0], FIRST)
    at_east = -face(own[1], east, FIRST)
    at_south = face(south, own[2], SECOND)
    at_north = -face(own[3], north, SECOND)
    low[...] = partial[:, :8]
    high[...] = partial[:, cols - 8 :]
    for held, r, term in ((top, 0, at_west), (bottom, rows - 1, at_east)):
        low[r] = low[r] + term[:8]
        held[...] = partial[r, 8 : cols - 8] + term[8 : cols - 8]
        high[r] = high[r] + term[cols - 8 :]
    low[:, 0, :] = low[:, 0, :] + at_south
    high[:, 7, :] = high[:, 7, :] + at_north
    places = [
        (low, (slice(None), first)),
        (high, (slice(None), final)),
        (top, (0, middle)),
        (bottom, (rows - 1, middle)),
    ]
    writes = [
        pltpu.make_async_copy(held, out.at[p], sems.at[k]) for k, (held, p) in enumerate(places)
    ]
    for copy in writes:
        copy.start()
    for copy in writes:
        copy.wait()
    inside.wait()


def in_vmem():
    return pl.BlockSpec(memory_space=pltpu.VMEM)


def in_hbm():
    return pl.BlockSpec(memory_space=pltpu.HBM)


def anywhere():
    return pl.BlockSpec(memory_space=pl.ANY)


def kept_in_hbm(x):
    return pltpu.with_memory_space_constraint(x, pltpu.HBM)


def vmem_array(shape, dtype):
    return pltpu.VMEM(shape, dtype)


def kept_in_vmem(x):
    return pltpu.with_memory_space_constraint(x, pltpu.VMEM)


def packed(air_state, edge_map, n_x, n_y):
    rows, cols, feat = air_state.shape
    return pl.pallas_call(
        functools.partial(pack_kernel, n_x, n_y),
        out_shape=[vmem_array((4, cols, feat), jnp.float32)]
        + [vmem_array((cols, feat), jnp.float32)] * 7,
        in_specs=[in_hbm()] * 2,
        out_specs=[in_vmem()] * 8,
        scratch_shapes=[
            pltpu.SMEM((3,) + edge_map.shape[1:], jnp.int32),
            pltpu.SemaphoreType.DMA((7,)),
        ],
        compiler_params=pltpu.CompilerParams(vmem_limit_bytes=4 * 1024 * 1024),
        name="own_edges",
    )(kept_in_hbm(air_state), kept_in_hbm(edge_map))


def idle_kernel(*refs):
    pass


def nothing(count):
    def make(*edges):
        x = edges[0]
        return tuple(
            pl.pallas_call(
                idle_kernel,
                out_shape=[jax.ShapeDtypeStruct(x.shape, x.dtype)] * count,
                in_specs=[anywhere()],
                out_specs=[anywhere()] * count,
                name="no_exchange",
            )(x)
        )

    return make


def interior(early, inputs, passed, started=(), groups=()):
    air_state = inputs[0]
    held = []
    for k, x in enumerate(inputs):
        space = pltpu.SMEM if k == 1 else pltpu.VMEM
        held.append(space(x.shape[1:] if k == 1 else x.shape, x.dtype))
    like = lambda x: vmem_array(x.shape, x.dtype)
    outs = [vmem_array(air_state.shape, jnp.float32)]
    outs += [like(x) for x in started[1:]]
    n_in, n_passed, n_started = len(inputs), len(passed), len(started)
    targets = []
    for arrays, _, number in groups:
        targets.append(len(outs) if number is None else number)
        if number is None:
            outs.append(vmem_array((len(arrays),) + arrays[0].shape, arrays[0].dtype))
    every = [x for arrays, _, _ in groups for x in arrays]
    n_fixed = len(outs)
    aliases = {n_in + k: n_fixed + k for k in range(n_passed)}
    aliases.update({n_in + n_passed + k: k for k in range(n_started)})
    rows, cols, feat = air_state.shape
    tiles = rows * cols // TILE

    def kernel(*refs):
        refs = list(refs)
        n_before = n_in + n_passed + n_started
        results = refs[n_before + len(every) :][: n_fixed + n_passed]
        rest = refs[n_before + len(every) + len(results) :]
        moved, at = [], n_before
        for (arrays, wanted, _), target in zip(groups, targets):
            moved.append((refs[at : at + len(arrays)], results[target], wanted))
            at += len(arrays)
        main_kernel(early, refs[:n_in], moved, results[0], (rest[:n_in], *rest[n_in:]))

    return pl.pallas_call(
        kernel,
        out_shape=outs + [like(x) for x in passed],
        in_specs=[in_hbm()] * n_in
        + [in_vmem()] * (n_passed + n_started)
        + [anywhere()] * len(every),
        out_specs=[in_vmem()] * (n_fixed + n_passed),
        scratch_shapes=held
        + [
            pltpu.SemaphoreType.DMA((n_in,)),
            pltpu.SemaphoreType.DMA((max(len(every), 1),)),
            pltpu.VMEM((rows * cols + TILE, feat), jnp.bfloat16),
            pltpu.VMEM((rows * cols + TILE, feat), jnp.float32),
            pltpu.SMEM((tiles + GROUP,), jnp.int32),
            pltpu.VMEM((6, rows, 4, cols // 4, feat), jnp.float32),
        ],
        input_output_aliases=aliases,
        compiler_params=pltpu.CompilerParams(vmem_limit_bytes=32 * 1024 * 1024),
        cost_estimate=pl.CostEstimate(
            flops=1_000_000_000, bytes_accessed=4_200_000, transcendentals=1_000_000
        ),
        name="columns_ahead" if early else "columns_behind",
    )(*map(kept_in_hbm, inputs), *map(kept_in_vmem, (*passed, *started)), *every)


def collected(arrays, wanted, passed):
    count, n_passed = len(arrays), len(passed)
    like = lambda x: vmem_array(x.shape, x.dtype)

    def kernel(*refs):
        row = lax.axis_index("gx")
        sources, target, sems = refs[:count], refs[count + n_passed], refs[-1]
        end_moves(start_moves([(sources, target, wanted)], sems, row), row)

    return pl.pallas_call(
        kernel,
        out_shape=[vmem_array((count,) + arrays[0].shape, arrays[0].dtype)]
        + [like(x) for x in passed],
        in_specs=[anywhere()] * count + [in_vmem()] * n_passed,
        out_specs=[in_vmem()] * (1 + n_passed),
        scratch_shapes=[pltpu.SemaphoreType.DMA((count,))],
        input_output_aliases={count + k: 1 + k for k in range(n_passed)},
        name="early_traces",
    )(*arrays, *map(kept_in_vmem, passed))


def boundary(edges, early, late, from_low, from_high, partial):
    rows, cols, feat = partial.shape
    return pl.pallas_call(
        edge_kernel,
        out_shape=jax.ShapeDtypeStruct(partial.shape, jnp.float32),
        in_specs=[in_vmem()] * 6,
        out_specs=in_hbm(),
        scratch_shapes=[
            pltpu.VMEM((rows, 8, feat), jnp.float32),
            pltpu.VMEM((rows, 8, feat), jnp.float32),
            pltpu.VMEM((cols - 16, feat), jnp.float32),
            pltpu.VMEM((cols - 16, feat), jnp.float32),
            pltpu.SemaphoreType.DMA((5,)),
        ],
        compiler_params=pltpu.CompilerParams(vmem_limit_bytes=8 * 1024 * 1024),
        cost_estimate=pl.CostEstimate(flops=2_000_000, bytes_accessed=600_000, transcendentals=0),
        name="boundary_faces",
    )(edges, early, late, from_low, from_high, partial)


def swap(rows, cols, n_y):
    pairs = []
    for r, other_r in rows:
        for c, other_c in cols:
            one, two = r * n_y + c, other_r * n_y + other_c
            pairs += [(one, two), (two, one)]
    return pairs


def on_device(
    air_state,
    edge_map,
    tile_class,
    in_weight,
    in_bias,
    mid_weight,
    mid_bias,
    out_weight,
    land_in,
    land_bias,
    land_out,
):
    n_x, n_y = lax.axis_size("gx"), lax.axis_size("gy")
    inputs = (
        air_state,
        tile_class,
        in_weight,
        in_bias.reshape(1, -1),
        mid_weight,
        mid_bias.reshape(1, -1),
        out_weight,
        land_in,
        land_bias.reshape(1, -1),
        land_out,
    )
    row = lax.axis_index("gx")
    late = [i for i in range(n_x) if i % WRAP == WRAP - 1]
    early = [i for i in range(n_x) if i not in late]
    evens = [(i, i + 1) for i in range(0, n_x, 2)]
    odds = [(i, (i + 1) % n_x) for i in range(1, n_x, 2)]
    col_evens = [(j, j + 1) for j in range(0, n_y, 2)]
    col_odds = [(j, (j + 1) % n_y) for j in range(1, n_y, 2)]
    col_same = [(j, j) for j in range(n_y)]

    def move(x, rows, cols):
        return lax.ppermute(x, ("gx", "gy"), swap(rows, cols, n_y))

    def exchange_early(row_even, row_odd, col_odd, col_even):
        same = [(i, i) for i in early]
        return (
            move(col_even, same, col_evens),
            move(col_odd, same, col_odds),
            move(row_odd, [p for p in odds if p[0] not in late], col_same),
            move(row_even, [p for p in evens if p[1] not in late], col_same),
        )

    def exchange_late_cols(col_odd, col_even):
        same = [(i, i) for i in late]
        return move(col_even, same, col_evens), move(col_odd, same, col_odds)

    def exchange_late_rows(row_even):
        return (move(row_even, [p for p in evens if p[1] in late], col_same),)

    def across(x, rows):
        return lax.ppermute(
            x, ("gx", "gy"), [(a * n_y + j, b * n_y + j) for a, b in rows for j in range(n_y)]
        )

    place = row % WRAP
    wraps = [p for p in odds if p[0] in late]
    is_first = lambda r: r % WRAP == 0
    is_middle = lambda r: (r % WRAP > 0) & (r % WRAP < WRAP - 1)
    is_late = lambda r: r % WRAP >= WRAP - 2
    own, late_even, wrap, row_even, row_odd, col_even, col_odd, back = packed(
        air_state, edge_map.transpose(0, 2, 1), n_x, n_y
    )
    partial, wrap, row_even, row_odd, col_even, col_odd, back = interior(
        True, inputs, (wrap, row_even, row_odd, col_even, col_odd, back)
    )
    from_low = across(wrap, wraps)
    early_traces = lax.cond(
        place < WRAP - 1, exchange_early, nothing(4), row_even, row_odd, col_odd, col_even
    )
    early_held, back, late_even = collected(early_traces, is_first, (back, late_even))
    from_high = across(back, [(b, a) for a, b in wraps])
    late_cols = lax.cond(
        place == WRAP - 1, exchange_late_cols, nothing(2), col_odd, col_even
    )
    late_rows = lax.cond(place >= WRAP - 2, exchange_late_rows, nothing(1), late_even)
    partial, early_held, late_held = interior(
        False,
        inputs,
        (),
        (partial, early_held),
        ((early_traces, is_middle, 1), ((*late_cols, *late_rows), is_late, None)),
    )
    return boundary(own, early_held, late_held, from_low, from_high, partial)


def solution(mesh):
    row_split, col_split = P("gx", "gy", None), P(None, "gy", None)
    return jax.shard_map(
        on_device,
        mesh=mesh,
        in_specs=(row_split, P(), col_split) + (P(),) * 8,
        out_specs=row_split,
        check_vma=False,
    )
```

```python
import functools
import math

import jax
import jax.numpy as jnp
import numpy as np
from jax import lax
from jax.experimental import pallas as pl
from jax.experimental.pallas import tpu as pltpu
from jax.sharding import PartitionSpec as P

CHUNK = 16
TILE = 64
GROUP = 8
WRAP = 8
FIRST, SECOND = "first", "second"


def lobatto_derivative():
    points = np.array([-1.0, -math.sqrt(0.2), math.sqrt(0.2), 1.0])
    barycentric = np.array(
        [1.0 / np.prod([points[j] - points[k] for k in range(4) if k != j]) for j in range(4)]
    )
    derivative = np.zeros((4, 4))
    for i in range(4):
        for j in range(4):
            if i != j:
                derivative[i, j] = barycentric[j] / barycentric[i] / (points[i] - points[j])
        derivative[i, i] = -np.sum([derivative[i, k] for k in range(4) if k != i])
    return derivative


def lane_block(shape):
    return lax.broadcasted_iota(jnp.int32, shape, len(shape) - 1) // 32


def spread(values, block, source):
    axis = values.ndim - 1
    if source == 0:
        once = jnp.where(block == 0, values, pltpu.roll(values, 32, axis))
        return jnp.where(block < 2, once, pltpu.roll(once, 64, axis))
    if source == 1:
        once = jnp.where(block == 1, values, pltpu.roll(values, 96, axis))
        return jnp.where(block < 2, once, pltpu.roll(once, 64, axis))
    once = jnp.where(block == 2, values, pltpu.roll(values, 32, axis))
    return jnp.where(block >= 2, once, pltpu.roll(once, 64, axis))


def primitives(states):
    flat = states.reshape(-1, states.shape[-1])
    block = lane_block(flat.shape)
    density = spread(flat, block, 0)
    carried = flat / density
    first = spread(carried, block, 1)
    second = spread(carried, block, 2)
    carried = jnp.where(block == 0, 1.0, carried)
    half_pressure = 0.25 * flat
    zero = jnp.zeros_like(flat)
    pressure_first = jnp.where(block == 1, pltpu.roll(half_pressure, 64, 1), zero)
    pressure_second = jnp.where(block == 2, pltpu.roll(half_pressure, 96, 1), zero)
    back = lambda x: x.reshape(states.shape)
    return {
        "q": states,
        "d": back(density),
        "c": back(carried),
        FIRST: (back(0.125 * first), back(pressure_first)),
        SECOND: (back(0.125 * second), back(pressure_second)),
    }


def pick(prims, index):
    out = {k: prims[k][index] for k in ("q", "d", "c")}
    for k in (FIRST, SECOND):
        out[k] = tuple(x[index] for x in prims[k])
    return out


def flux(one, two, axis):
    return (one["d"] + two["d"]) * (one[axis][0] + two[axis][0]) * (one["c"] + two["c"]) + (
        one[axis][1] + two[axis][1]
    )


def face(left, right, axis):
    wave = 8.0 * jnp.maximum(jnp.abs(left[axis][0]), jnp.abs(right[axis][0])) + 1.0
    return 6.0 * flux(left, right, axis) - (3.0 * wave) * (right["q"] - left["q"])


def volume(nodes, axis):
    derivative = lobatto_derivative()
    fluxes = {}
    for a in range(4):
        for b in range(a + 1, 4):
            fluxes[a, b] = fluxes[b, a] = flux(nodes[a], nodes[b], axis)
    results = []
    for a in range(4):
        total = None
        for b in range(4):
            if b != a:
                term = (-2.0 * float(derivative[a, b])) * fluxes[a, b]
                total = term if total is None else total + term
        results.append(total)
    return results


def silu(z):
    half = 0.5 * z
    return (half + half * jnp.tanh(half)).astype(jnp.bfloat16)


def dot(a, b):
    return jnp.dot(a, b, preferred_element_type=jnp.float32)


def ahead(row, col):
    return ((row % WRAP == 0) & ((row > 0) | (col > 0))) | ((row == 1) & (col == 0))


def turned(edge):
    count = edge.shape[0] // 8
    place = lax.broadcasted_iota(jnp.int32, (8, edge.shape[1]), 0)
    pieces = []
    for k in range(count):
        piece = edge[(count - 1 - k) * 8 : (count - k) * 8]
        piece = pltpu.roll(piece, 4, 0)
        piece = jnp.where(place % 4 < 2, pltpu.roll(piece, 6, 0), pltpu.roll(piece, 2, 0))
        piece = jnp.where(place % 2 < 1, pltpu.roll(piece, 7, 0), pltpu.roll(piece, 1, 0))
        pieces.append(piece)
    return jnp.concatenate(pieces, axis=0)


def pack_kernel(n_x, n_y, air, edge_map, own, late_even, wrap, row_even, col_even, col_odd, back, maps, sems):
    rows, cols, _ = air.shape
    row, col = lax.axis_index("gx"), lax.axis_index("gy")
    west, east = (row + n_x - 1) % n_x, (row + 1) % n_x
    south, north = (col + n_y - 1) % n_y, (col + 1) % n_y
    copies = [
        pltpu.make_async_copy(air.at[:, 0], own.at[2], sems.at[0]),
        pltpu.make_async_copy(air.at[:, cols - 1], own.at[3], sems.at[1]),
        pltpu.make_async_copy(air.at[0], own.at[0], sems.at[2]),
        pltpu.make_async_copy(air.at[rows - 1], own.at[1], sems.at[3]),
        pltpu.make_async_copy(edge_map.at[west], maps.at[0], sems.at[4]),
        pltpu.make_async_copy(edge_map.at[row], maps.at[1], sems.at[5]),
        pltpu.make_async_copy(edge_map.at[east], maps.at[2], sems.at[6]),
    ]
    for copy in copies:
        copy.start()
    for copy in copies:
        copy.wait()

    def asked(code):
        edge = own[code % 4]
        return jnp.where(code >= 4, turned(edge), edge)

    to_west = asked(maps[0, 1, col])
    to_east = asked(maps[2, 0, col])
    to_south = asked(maps[1, 3, south])
    to_north = asked(maps[1, 2, north])
    even = row % 2 == 0
    row_even[...] = jnp.where(even, to_east, to_west)
    odd = jnp.where(even, to_west, to_east)
    late_even[...] = row_even[...]
    back[...] = odd
    even = col % 2 == 0
    paired = jnp.where(even, to_north, to_south)
    col_even[...] = paired
    beside = (row % WRAP == 0) | (row % WRAP == WRAP - 1)
    wrap[...] = jnp.where(beside, odd, paired)
    col_odd[...] = jnp.where(even, to_south, to_north)


def main_kernel(early, inputs, moved, result, scratch):
    held, sems, move_sems, normed, base, listed, fields = scratch
    row = lax.axis_index("gx")
    col = lax.axis_index("gy")
    moves = start_moves(moved, move_sems, row)

    @pl.when(ahead(row, col) == early)
    def _():
        copies = []
        for k, (source, target) in enumerate(zip(inputs, held)):
            if k == 1:
                source = source.at[row]
            copies.append(pltpu.make_async_copy(source, target, sems.at[k]))
        for k in (0, 2, 3, 6, 1, 7, 8, 4, 5, 9):
            copies[k].start()

        def ready(*numbers):
            for k in numbers:
                copies[k].wait()

        columns_and_interior(held, ready, normed, base, listed, fields, result)

    end_moves(moves, row)


def start_moves(moved, sems, row):
    moves = []
    for sources, target, wanted in moved:
        first = sum(len(copies) for copies, _ in moves)
        copies = [
            pltpu.make_async_copy(ref, target.at[k], sems.at[first + k])
            for k, ref in enumerate(sources)
        ]
        moves.append((copies, wanted))
    for copies, wanted in moves:

        @pl.when(wanted(row))
        def _():
            for copy in copies:
                copy.start()

    return moves


def end_moves(moves, row):
    for copies, wanted in moves:

        @pl.when(wanted(row))
        def _():
            for copy in copies:
                copy.wait()


def two_layers(x, weight, bias, last):
    return dot(silu(dot(x, weight[...]) + bias[...]), last[...])


def columns_and_interior(held, ready, normed_ref, base, listed, fields, out):
    air, classes, in_w, in_b, mid_w, mid_b, out_w, land_in, land_b, land_out = held
    rows, cols, feat = air.shape
    tiles = rows * cols // TILE
    chunk_cols = CHUNK * cols

    ready(0, 2, 3, 6)

    def base_chunk(c, carry):
        start = pl.multiple_of(c * CHUNK, CHUNK)
        columns = air[pl.ds(start, CHUNK)].reshape(chunk_cols, feat).astype(jnp.bfloat16)
        values = columns.astype(jnp.float32)
        mean = jnp.sum(values * values, axis=-1, keepdims=True) * (1.0 / feat)
        normed = (values * lax.rsqrt(mean + 1e-06)).astype(jnp.bfloat16)
        place = pl.ds(pl.multiple_of(c * chunk_cols, chunk_cols), chunk_cols)
        normed_ref[place, :] = normed
        base[place, :] = two_layers(normed, in_w, in_b, out_w)
        store_fields(start, CHUNK, air, fields)
        return carry

    lax.fori_loop(0, rows // CHUNK, base_chunk, 0)

    ready(1)

    def note(t, count):
        listed[count] = t
        return count + classes[0, t]

    lands = lax.fori_loop(0, tiles, note, 0)
    for k in range(GROUP):
        listed[lands + k] = tiles

    @pl.when(lands > 0)
    def _():
        ready(4, 5, 7, 8, 9)

    def land_group(first, count):
        starts = [pl.multiple_of(listed[first + k] * TILE, TILE) for k in range(count)]
        normed = jnp.concatenate([normed_ref[pl.ds(s, TILE), :] for s in starts], axis=0)
        land = silu(dot(normed, land_in[...]) + land_b[...])
        term = two_layers(land, mid_w, mid_b, land_out)
        for k, s in enumerate(starts):
            base[pl.ds(s, TILE), :] = base[pl.ds(s, TILE), :] + term[k * TILE : (k + 1) * TILE]

    def whole_group(g, carry):
        land_group(g * GROUP, GROUP)
        return carry

    half = GROUP // 2
    over = lands % GROUP
    whole = lands // GROUP + jnp.where(over > half, 1, 0)
    lax.fori_loop(0, whole, whole_group, 0)

    @pl.when((over > 0) & (over <= half))
    def _():
        land_group(whole * GROUP, half)

    interior_and_sum(air, fields, base, out)

    @pl.when(lands == 0)
    def _():
        ready(4, 5, 7, 8, 9)


def store_fields(start, count, air, fields):
    _, cols, feat = air.shape
    elements = cols // 4
    for a in range(4):
        states = air[pl.ds(start, count), pl.ds(a, elements, stride=4), :]
        flat = states.reshape(-1, feat)
        block = lane_block(flat.shape)
        density = spread(flat, block, 0)
        carried = flat * pl.reciprocal(density)
        speeds = 0.125 * carried
        half_pressure = 0.25 * flat
        values = (
            density,
            jnp.where(block == 0, 1.0, carried),
            spread(speeds, block, 1),
            spread(speeds, block, 2),
            jnp.where(block == 1, pltpu.roll(half_pressure, 64, 1), 0.0),
            jnp.where(block == 2, pltpu.roll(half_pressure, 96, 1), 0.0),
        )
        for k, value in enumerate(values):
            fields[k, pl.ds(start, count), a] = value.reshape(states.shape)


def node_fields(fields, row, a):
    d, c, u, v, p, s = (fields[k, row, a] for k in range(6))
    return {"d": d, "c": c, "q": d * c, FIRST: (u, p), SECOND: (v, s)}


def interior_and_sum(air, fields, base, out):
    rows, cols, feat = air.shape
    elements = cols // 4
    count = rows // 4
    number = lax.broadcasted_iota(jnp.int32, (elements, feat), 0)

    def element(e, below):
        start = e * 4
        after = jnp.minimum(start + 4, rows - 1)
        inside = jnp.where(e < count - 1, 1.0, 0.0)
        sums = [[None] * 4 for _ in range(4)]
        above = []
        for a in range(4):
            nodes = [node_fields(fields, start + r, a) for r in range(4)]
            totals = volume(nodes, FIRST)
            high = inside * face(nodes[3], node_fields(fields, after, a), FIRST)
            above.append(high)
            totals[0] = totals[0] + below[a]
            totals[3] = totals[3] - high
            for r in range(4):
                sums[r][a] = totals[r]
        for r in range(4):
            nodes = [node_fields(fields, start + r, a) for a in range(4)]
            totals = volume(nodes, SECOND)
            lower = jax.tree.map(lambda x: pltpu.roll(x, 1, 0), nodes[3])
            faces = jnp.where(number == 0, 0.0, face(lower, nodes[0], SECOND))
            totals[0] = totals[0] + faces
            totals[3] = totals[3] - pltpu.roll(faces, elements - 1, 0)
            for a in range(4):
                along = pl.ds(a, elements, stride=4)
                out[start + r, along, :] = sums[r][a] + totals[a]
        physics = base[pl.ds(pl.multiple_of(start * cols, 4 * cols), 4 * cols), :]
        physics = physics.astype(jnp.bfloat16).astype(jnp.float32).reshape(4, cols, feat)
        out[pl.ds(start, 4)] = out[pl.ds(start, 4)] + physics
        return tuple(above)

    zero = jnp.zeros((elements, feat), jnp.float32)
    lax.fori_loop(0, count, element, (zero,) * 4)


def edge_kernel(edges, early, late, from_low, from_high, partial, out, low, high, top, bottom, sems):
    col_odd_a, row_even_a, col_even_first = (early[k] for k in range(3))
    col_even_b, col_odd_b, row_even_b = (late[k] for k in range(3))
    rows, cols, feat = out.shape
    first, middle, final = pl.ds(0, 8), pl.ds(8, cols - 16), pl.ds(cols - 8, 8)
    inner = (pl.ds(1, rows - 2), middle)
    inside = pltpu.make_async_copy(partial.at[inner], out.at[inner], sems.at[4])
    inside.start()
    row, col = lax.axis_index("gx"), lax.axis_index("gy")
    place = row % WRAP
    last_row = place == WRAP - 1
    first_x = jnp.where(place < WRAP - 2, row_even_a, row_even_b)
    second_x = jnp.where(place == 0, from_low[...], from_high[...])
    even = row % 2 == 0
    west = jnp.where(even, second_x, first_x)
    east = jnp.where(even, first_x, second_x)
    first_y = jnp.where(place == 0, col_even_first, from_low[...])
    first_y = jnp.where(last_row, col_even_b, first_y)
    second_y = jnp.where(last_row, col_odd_b, col_odd_a)
    even = col % 2 == 0
    south = jnp.where(even, second_y, first_y)
    north = jnp.where(even, first_y, second_y)
    own = [primitives(edges[s]) for s in range(4)]
    west, east, south, north = (primitives(x) for x in (west, east, south, north))
    at_west = face(west, own[0], FIRST)
    at_east = -face(own[1], east, FIRST)
    at_south = face(south, own[2], SECOND)
    at_north = -face(own[3], north, SECOND)
    low[...] = partial[:, :8]
    high[...] = partial[:, cols - 8 :]
    for held, r, term in ((top, 0, at_west), (bottom, rows - 1, at_east)):
        low[r] = low[r] + term[:8]
        held[...] = partial[r, 8 : cols - 8] + term[8 : cols - 8]
        high[r] = high[r] + term[cols - 8 :]
    low[:, 0, :] = low[:, 0, :] + at_south
    high[:, 7, :] = high[:, 7, :] + at_north
    places = [
        (low, (slice(None), first)),
        (high, (slice(None), final)),
        (top, (0, middle)),
        (bottom, (rows - 1, middle)),
    ]
    writes = [
        pltpu.make_async_copy(held, out.at[p], sems.at[k]) for k, (held, p) in enumerate(places)
    ]
    for copy in writes:
        copy.start()
    for copy in writes:
        copy.wait()
    inside.wait()


def in_vmem():
    return pl.BlockSpec(memory_space=pltpu.VMEM)


def in_hbm():
    return pl.BlockSpec(memory_space=pltpu.HBM)


def anywhere():
    return pl.BlockSpec(memory_space=pl.ANY)


def kept_in_hbm(x):
    return pltpu.with_memory_space_constraint(x, pltpu.HBM)


def vmem_array(shape, dtype):
    return pltpu.VMEM(shape, dtype)


def kept_in_vmem(x):
    return pltpu.with_memory_space_constraint(x, pltpu.VMEM)


def packed(air_state, edge_map, n_x, n_y):
    rows, cols, feat = air_state.shape
    return pl.pallas_call(
        functools.partial(pack_kernel, n_x, n_y),
        out_shape=[vmem_array((4, cols, feat), jnp.float32)]
        + [vmem_array((cols, feat), jnp.float32)] * 6,
        in_specs=[in_hbm()] * 2,
        out_specs=[in_vmem()] * 7,
        scratch_shapes=[
            pltpu.SMEM((3,) + edge_map.shape[1:], jnp.int32),
            pltpu.SemaphoreType.DMA((7,)),
        ],
        compiler_params=pltpu.CompilerParams(vmem_limit_bytes=4 * 1024 * 1024),
        name="own_edges",
    )(kept_in_hbm(air_state), kept_in_hbm(edge_map))


def idle_kernel(*refs):
    pass


def nothing(count):
    def make(*edges):
        x = edges[0]
        return tuple(
            pl.pallas_call(
                idle_kernel,
                out_shape=[jax.ShapeDtypeStruct(x.shape, x.dtype)] * count,
                in_specs=[anywhere()],
                out_specs=[anywhere()] * count,
                name="no_exchange",
            )(x)
        )

    return make


def interior(early, inputs, passed, started=(), groups=()):
    air_state = inputs[0]
    held = []
    for k, x in enumerate(inputs):
        space = pltpu.SMEM if k == 1 else pltpu.VMEM
        held.append(space(x.shape[1:] if k == 1 else x.shape, x.dtype))
    like = lambda x: vmem_array(x.shape, x.dtype)
    outs = [vmem_array(air_state.shape, jnp.float32)]
    outs += [like(x) for x in started[1:]]
    n_in, n_passed, n_started = len(inputs), len(passed), len(started)
    targets = []
    for arrays, _, number in groups:
        targets.append(len(outs) if number is None else number)
        if number is None:
            outs.append(vmem_array((len(arrays),) + arrays[0].shape, arrays[0].dtype))
    every = [x for arrays, _, _ in groups for x in arrays]
    n_fixed = len(outs)
    aliases = {n_in + k: n_fixed + k for k in range(n_passed)}
    aliases.update({n_in + n_passed + k: k for k in range(n_started)})
    rows, cols, feat = air_state.shape
    tiles = rows * cols // TILE

    def kernel(*refs):
        refs = list(refs)
        n_before = n_in + n_passed + n_started
        results = refs[n_before + len(every) :][: n_fixed + n_passed]
        rest = refs[n_before + len(every) + len(results) :]
        moved, at = [], n_before
        for (arrays, wanted, _), target in zip(groups, targets):
            moved.append((refs[at : at + len(arrays)], results[target], wanted))
            at += len(arrays)
        main_kernel(early, refs[:n_in], moved, results[0], (rest[:n_in], *rest[n_in:]))

    return pl.pallas_call(
        kernel,
        out_shape=outs + [like(x) for x in passed],
        in_specs=[in_hbm()] * n_in
        + [in_vmem()] * (n_passed + n_started)
        + [anywhere()] * len(every),
        out_specs=[in_vmem()] * (n_fixed + n_passed),
        scratch_shapes=held
        + [
            pltpu.SemaphoreType.DMA((n_in,)),
            pltpu.SemaphoreType.DMA((max(len(every), 1),)),
            pltpu.VMEM((rows * cols + TILE, feat), jnp.bfloat16),
            pltpu.VMEM((rows * cols + TILE, feat), jnp.float32),
            pltpu.SMEM((tiles + GROUP,), jnp.int32),
            pltpu.VMEM((6, rows, 4, cols // 4, feat), jnp.float32),
        ],
        input_output_aliases=aliases,
        compiler_params=pltpu.CompilerParams(vmem_limit_bytes=32 * 1024 * 1024),
        cost_estimate=pl.CostEstimate(
            flops=1_000_000_000, bytes_accessed=4_200_000, transcendentals=1_000_000
        ),
        name="columns_ahead" if early else "columns_behind",
    )(*map(kept_in_hbm, inputs), *map(kept_in_vmem, (*passed, *started)), *every)


def collected(arrays, wanted, passed):
    count, n_passed = len(arrays), len(passed)
    like = lambda x: vmem_array(x.shape, x.dtype)

    def kernel(*refs):
        row = lax.axis_index("gx")
        sources, target, sems = refs[:count], refs[count + n_passed], refs[-1]
        end_moves(start_moves([(sources, target, wanted)], sems, row), row)

    return pl.pallas_call(
        kernel,
        out_shape=[vmem_array((count,) + arrays[0].shape, arrays[0].dtype)]
        + [like(x) for x in passed],
        in_specs=[anywhere()] * count + [in_vmem()] * n_passed,
        out_specs=[in_vmem()] * (1 + n_passed),
        scratch_shapes=[pltpu.SemaphoreType.DMA((count,))],
        input_output_aliases={count + k: 1 + k for k in range(n_passed)},
        name="early_traces",
    )(*arrays, *map(kept_in_vmem, passed))


def boundary(edges, early, late, from_low, from_high, partial):
    rows, cols, feat = partial.shape
    return pl.pallas_call(
        edge_kernel,
        out_shape=jax.ShapeDtypeStruct(partial.shape, jnp.float32),
        in_specs=[in_vmem()] * 6,
        out_specs=in_hbm(),
        scratch_shapes=[
            pltpu.VMEM((rows, 8, feat), jnp.float32),
            pltpu.VMEM((rows, 8, feat), jnp.float32),
            pltpu.VMEM((cols - 16, feat), jnp.float32),
            pltpu.VMEM((cols - 16, feat), jnp.float32),
            pltpu.SemaphoreType.DMA((5,)),
        ],
        compiler_params=pltpu.CompilerParams(vmem_limit_bytes=8 * 1024 * 1024),
        cost_estimate=pl.CostEstimate(flops=2_000_000, bytes_accessed=600_000, transcendentals=0),
        name="boundary_faces",
    )(edges, early, late, from_low, from_high, partial)


def swap(rows, cols, n_y):
    pairs = []
    for r, other_r in rows:
        for c, other_c in cols:
            one, two = r * n_y + c, other_r * n_y + other_c
            pairs += [(one, two), (two, one)]
    return pairs


def on_device(
    air_state,
    edge_map,
    tile_class,
    in_weight,
    in_bias,
    mid_weight,
    mid_bias,
    out_weight,
    land_in,
    land_bias,
    land_out,
):
    n_x, n_y = lax.axis_size("gx"), lax.axis_size("gy")
    inputs = (
        air_state,
        tile_class,
        in_weight,
        in_bias.reshape(1, -1),
        mid_weight,
        mid_bias.reshape(1, -1),
        out_weight,
        land_in,
        land_bias.reshape(1, -1),
        land_out,
    )
    row = lax.axis_index("gx")
    late = [i for i in range(n_x) if i % WRAP == WRAP - 1]
    early = [i for i in range(n_x) if i not in late]
    first = [i for i in early if i % WRAP == 0]
    inner = [i for i in early if i not in first]
    evens = [(i, i + 1) for i in range(0, n_x, 2)]
    odds = [(i, (i + 1) % n_x) for i in range(1, n_x, 2)]
    col_evens = [(j, j + 1) for j in range(0, n_y, 2)]
    col_odds = [(j, (j + 1) % n_y) for j in range(1, n_y, 2)]
    col_same = [(j, j) for j in range(n_y)]

    def move(x, rows, cols):
        return lax.ppermute(x, ("gx", "gy"), swap(rows, cols, n_y))

    def exchange_early(col_odd, row_even):
        same = [(i, i) for i in early]
        return (
            move(col_odd, same, col_odds),
            move(row_even, [p for p in evens if p[1] not in late], col_same),
        )

    def exchange_first(col_even):
        return (move(col_even, [(i, i) for i in first], col_evens),)

    def exchange_late_cols(col_odd, col_even):
        same = [(i, i) for i in late]
        return move(col_even, same, col_evens), move(col_odd, same, col_odds)

    def exchange_late_rows(row_even):
        return (move(row_even, [p for p in evens if p[1] in late], col_same),)

    def across(x, rows, others, cols):
        pairs = [(a * n_y + j, b * n_y + j) for a, b in rows for j in range(n_y)]
        return lax.ppermute(x, ("gx", "gy"), pairs + swap(others, cols, n_y))

    place = row % WRAP
    wraps = [p for p in odds if p[0] in late]
    is_first = lambda r: r % WRAP == 0
    is_middle = lambda r: (r % WRAP > 0) & (r % WRAP < WRAP - 1)
    is_late = lambda r: r % WRAP >= WRAP - 2
    own, late_even, wrap, row_even, col_even, col_odd, back = packed(
        air_state, edge_map.transpose(0, 2, 1), n_x, n_y
    )
    partial, wrap, row_even, col_even, col_odd, back = interior(
        True, inputs, (wrap, row_even, col_even, col_odd, back)
    )
    from_low = across(wrap, wraps, [(i, i) for i in inner], col_evens)
    first_traces = lax.cond(place == 0, exchange_first, nothing(1), col_even)
    early_traces = lax.cond(place < WRAP - 1, exchange_early, nothing(2), col_odd, row_even)
    early_traces = (*early_traces, *first_traces)
    early_held, back, late_even = collected(early_traces, is_first, (back, late_even))
    from_high = across(
        back, [(b, a) for a, b in wraps], [p for p in odds if p[0] not in late], col_same
    )
    late_cols = lax.cond(
        place == WRAP - 1, exchange_late_cols, nothing(2), col_odd, col_even
    )
    late_rows = lax.cond(place >= WRAP - 2, exchange_late_rows, nothing(1), late_even)
    partial, early_held, late_held = interior(
        False,
        inputs,
        (),
        (partial, early_held),
        ((early_traces, is_middle, 1), ((*late_cols, *late_rows), is_late, None)),
    )
    return boundary(own, early_held, late_held, from_low, from_high, partial)


def solution(mesh):
    row_split, col_split = P("gx", "gy", None), P(None, "gy", None)
    return jax.shard_map(
        on_device,
        mesh=mesh,
        in_specs=(row_split, P(), col_split) + (P(),) * 8,
        out_specs=row_split,
        check_vma=False,
    )
```

```python
import functools
import math

import jax
import jax.numpy as jnp
import numpy as np
from jax import lax
from jax.experimental import pallas as pl
from jax.experimental.pallas import tpu as pltpu
from jax.sharding import PartitionSpec as P

CHUNK = 16
TILE = 64
RESIDENT = (0, 2, 3, 6)
GROUP = 8
WRAP = 8
FIRST, SECOND = "first", "second"


def lobatto_derivative():
    points = np.array([-1.0, -math.sqrt(0.2), math.sqrt(0.2), 1.0])
    barycentric = np.array(
        [1.0 / np.prod([points[j] - points[k] for k in range(4) if k != j]) for j in range(4)]
    )
    derivative = np.zeros((4, 4))
    for i in range(4):
        for j in range(4):
            if i != j:
                derivative[i, j] = barycentric[j] / barycentric[i] / (points[i] - points[j])
        derivative[i, i] = -np.sum([derivative[i, k] for k in range(4) if k != i])
    return derivative


def lane_block(shape):
    return lax.broadcasted_iota(jnp.int32, shape, len(shape) - 1) // 32


def spread(values, block, source):
    axis = values.ndim - 1
    if source == 0:
        once = jnp.where(block == 0, values, pltpu.roll(values, 32, axis))
        return jnp.where(block < 2, once, pltpu.roll(once, 64, axis))
    if source == 1:
        once = jnp.where(block == 1, values, pltpu.roll(values, 96, axis))
        return jnp.where(block < 2, once, pltpu.roll(once, 64, axis))
    once = jnp.where(block == 2, values, pltpu.roll(values, 32, axis))
    return jnp.where(block >= 2, once, pltpu.roll(once, 64, axis))


def primitives(states):
    flat = states.reshape(-1, states.shape[-1])
    block = lane_block(flat.shape)
    density = spread(flat, block, 0)
    carried = flat / density
    first = spread(carried, block, 1)
    second = spread(carried, block, 2)
    carried = jnp.where(block == 0, 1.0, carried)
    half_pressure = 0.25 * flat
    zero = jnp.zeros_like(flat)
    pressure_first = jnp.where(block == 1, pltpu.roll(half_pressure, 64, 1), zero)
    pressure_second = jnp.where(block == 2, pltpu.roll(half_pressure, 96, 1), zero)
    back = lambda x: x.reshape(states.shape)
    return {
        "q": states,
        "d": back(density),
        "c": back(carried),
        FIRST: (back(0.125 * first), back(pressure_first)),
        SECOND: (back(0.125 * second), back(pressure_second)),
    }


def pick(prims, index):
    out = {k: prims[k][index] for k in ("q", "d", "c")}
    for k in (FIRST, SECOND):
        out[k] = tuple(x[index] for x in prims[k])
    return out


def flux(one, two, axis):
    return (one["d"] + two["d"]) * (one[axis][0] + two[axis][0]) * (one["c"] + two["c"]) + (
        one[axis][1] + two[axis][1]
    )


def face(left, right, axis):
    wave = 8.0 * jnp.maximum(jnp.abs(left[axis][0]), jnp.abs(right[axis][0])) + 1.0
    return 6.0 * flux(left, right, axis) - (3.0 * wave) * (right["q"] - left["q"])


def volume(nodes, axis):
    derivative = lobatto_derivative()
    fluxes = {}
    for a in range(4):
        for b in range(a + 1, 4):
            fluxes[a, b] = fluxes[b, a] = flux(nodes[a], nodes[b], axis)
    results = []
    for a in range(4):
        total = None
        for b in range(4):
            if b != a:
                term = (-2.0 * float(derivative[a, b])) * fluxes[a, b]
                total = term if total is None else total + term
        results.append(total)
    return results


def silu(z):
    half = 0.5 * z
    return (half + half * jnp.tanh(half)).astype(jnp.bfloat16)


def dot(a, b):
    return jnp.dot(a, b, preferred_element_type=jnp.float32)


def ahead(row, col):
    return ((row % WRAP == 0) & ((row > 0) | (col > 0))) | ((row == 1) & (col == 0))


def turned(edge):
    count = edge.shape[0] // 8
    place = lax.broadcasted_iota(jnp.int32, (8, edge.shape[1]), 0)
    pieces = []
    for k in range(count):
        piece = edge[(count - 1 - k) * 8 : (count - k) * 8]
        piece = pltpu.roll(piece, 4, 0)
        piece = jnp.where(place % 4 < 2, pltpu.roll(piece, 6, 0), pltpu.roll(piece, 2, 0))
        piece = jnp.where(place % 2 < 1, pltpu.roll(piece, 7, 0), pltpu.roll(piece, 1, 0))
        pieces.append(piece)
    return jnp.concatenate(pieces, axis=0)


def pack_kernel(n_x, n_y, air_in, edge_map, *refs):
    fetched, refs = refs[: len(RESIDENT) - 1], refs[len(RESIDENT) - 1 :]
    air, *targets = refs[: len(RESIDENT)]
    own, late_even, wrap, row_even, col_even, col_odd, back, maps, sems = refs[len(RESIDENT) :]
    rows, cols, _ = air.shape
    row, col = lax.axis_index("gx"), lax.axis_index("gy")
    west, east = (row + n_x - 1) % n_x, (row + 1) % n_x
    south, north = (col + n_y - 1) % n_y, (col + 1) % n_y
    copies = [
        pltpu.make_async_copy(air_in, air, sems.at[0]),
        pltpu.make_async_copy(edge_map.at[west], maps.at[0], sems.at[1]),
        pltpu.make_async_copy(edge_map.at[row], maps.at[1], sems.at[2]),
        pltpu.make_async_copy(edge_map.at[east], maps.at[2], sems.at[3]),
    ]
    later = [
        pltpu.make_async_copy(source, target, sems.at[4 + k])
        for k, (source, target) in enumerate(zip(fetched, targets))
    ]
    for copy in copies + later:
        copy.start()
    for copy in copies:
        copy.wait()
    own[0] = air[0]
    own[1] = air[rows - 1]
    own[2] = air[:, 0, :]
    own[3] = air[:, cols - 1, :]

    def asked(code):
        edge = own[code % 4]
        return jnp.where(code >= 4, turned(edge), edge)

    to_west = asked(maps[0, 1, col])
    to_east = asked(maps[2, 0, col])
    to_south = asked(maps[1, 3, south])
    to_north = asked(maps[1, 2, north])
    even = row % 2 == 0
    row_even[...] = jnp.where(even, to_east, to_west)
    odd = jnp.where(even, to_west, to_east)
    late_even[...] = row_even[...]
    back[...] = odd
    even = col % 2 == 0
    paired = jnp.where(even, to_north, to_south)
    col_even[...] = paired
    beside = (row % WRAP == 0) | (row % WRAP == WRAP - 1)
    wrap[...] = jnp.where(beside, odd, paired)
    for copy in later:
        copy.wait()
    col_odd[...] = jnp.where(even, to_south, to_north)


def main_kernel(early, inputs, moved, result, scratch):
    held, sems, move_sems, normed, base, listed, fields = scratch
    row = lax.axis_index("gx")
    col = lax.axis_index("gy")
    moves = start_moves(moved, move_sems, row)

    @pl.when(ahead(row, col) == early)
    def _():
        copies = {}
        for k, (source, target) in enumerate(zip(inputs, held)):
            if k == 1:
                source = source.at[row]
            if k not in RESIDENT:
                copies[k] = pltpu.make_async_copy(source, target, sems.at[k])
        for k in (1, 7, 8, 4, 5, 9):
            copies[k].start()

        def ready(*numbers):
            for k in numbers:
                copies[k].wait()

        columns_and_interior(held, ready, normed, base, listed, fields, result)

    end_moves(moves, row)


def start_moves(moved, sems, row):
    moves = []
    for sources, target, wanted in moved:
        first = sum(len(copies) for copies, _ in moves)
        copies = [
            pltpu.make_async_copy(ref, target.at[k], sems.at[first + k])
            for k, ref in enumerate(sources)
        ]
        moves.append((copies, wanted))
    for copies, wanted in moves:

        @pl.when(wanted(row))
        def _():
            for copy in copies:
                copy.start()

    return moves


def end_moves(moves, row):
    for copies, wanted in moves:

        @pl.when(wanted(row))
        def _():
            for copy in copies:
                copy.wait()


def two_layers(x, weight, bias, last):
    return dot(silu(dot(x, weight[...]) + bias[...]), last[...])


def columns_and_interior(held, ready, normed_ref, base, listed, fields, out):
    air, classes, in_w, in_b, mid_w, mid_b, out_w, land_in, land_b, land_out = held
    rows, cols, feat = air.shape
    tiles = rows * cols // TILE
    chunk_cols = CHUNK * cols

    def base_chunk(c, carry):
        start = pl.multiple_of(c * CHUNK, CHUNK)
        columns = air[pl.ds(start, CHUNK)].reshape(chunk_cols, feat).astype(jnp.bfloat16)
        values = columns.astype(jnp.float32)
        mean = jnp.sum(values * values, axis=-1, keepdims=True) * (1.0 / feat)
        normed = (values * lax.rsqrt(mean + 1e-06)).astype(jnp.bfloat16)
        place = pl.ds(pl.multiple_of(c * chunk_cols, chunk_cols), chunk_cols)
        normed_ref[place, :] = normed
        base[place, :] = two_layers(normed, in_w, in_b, out_w)
        store_fields(start, CHUNK, air, fields)
        return carry

    lax.fori_loop(0, rows // CHUNK, base_chunk, 0)

    ready(1)

    def note(t, count):
        listed[count] = t
        return count + classes[0, t]

    lands = lax.fori_loop(0, tiles, note, 0)
    for k in range(GROUP):
        listed[lands + k] = tiles

    @pl.when(lands > 0)
    def _():
        ready(4, 5, 7, 8, 9)

    def land_group(first, count):
        starts = [pl.multiple_of(listed[first + k] * TILE, TILE) for k in range(count)]
        normed = jnp.concatenate([normed_ref[pl.ds(s, TILE), :] for s in starts], axis=0)
        land = silu(dot(normed, land_in[...]) + land_b[...])
        term = two_layers(land, mid_w, mid_b, land_out)
        for k, s in enumerate(starts):
            base[pl.ds(s, TILE), :] = base[pl.ds(s, TILE), :] + term[k * TILE : (k + 1) * TILE]

    def whole_group(g, carry):
        land_group(g * GROUP, GROUP)
        return carry

    half = GROUP // 2
    over = lands % GROUP
    whole = lands // GROUP + jnp.where(over > half, 1, 0)
    lax.fori_loop(0, whole, whole_group, 0)

    @pl.when((over > 0) & (over <= half))
    def _():
        land_group(whole * GROUP, half)

    interior_and_sum(air, fields, base, out)

    @pl.when(lands == 0)
    def _():
        ready(4, 5, 7, 8, 9)


def store_fields(start, count, air, fields):
    _, cols, feat = air.shape
    elements = cols // 4
    for a in range(4):
        states = air[pl.ds(start, count), pl.ds(a, elements, stride=4), :]
        flat = states.reshape(-1, feat)
        block = lane_block(flat.shape)
        density = spread(flat, block, 0)
        carried = flat * pl.reciprocal(density)
        speeds = 0.125 * carried
        half_pressure = 0.25 * flat
        values = (
            density,
            jnp.where(block == 0, 1.0, carried),
            spread(speeds, block, 1),
            spread(speeds, block, 2),
            jnp.where(block == 1, pltpu.roll(half_pressure, 64, 1), 0.0),
            jnp.where(block == 2, pltpu.roll(half_pressure, 96, 1), 0.0),
        )
        for k, value in enumerate(values):
            fields[k, pl.ds(start, count), a] = value.reshape(states.shape)


def node_fields(fields, row, a):
    d, c, u, v, p, s = (fields[k, row, a] for k in range(6))
    return {"d": d, "c": c, "q": d * c, FIRST: (u, p), SECOND: (v, s)}


def interior_and_sum(air, fields, base, out):
    rows, cols, feat = air.shape
    elements = cols // 4
    count = rows // 4
    number = lax.broadcasted_iota(jnp.int32, (elements, feat), 0)

    def element(e, below):
        start = e * 4
        after = jnp.minimum(start + 4, rows - 1)
        inside = jnp.where(e < count - 1, 1.0, 0.0)
        sums = [[None] * 4 for _ in range(4)]
        above = []
        for a in range(4):
            nodes = [node_fields(fields, start + r, a) for r in range(4)]
            totals = volume(nodes, FIRST)
            high = inside * face(nodes[3], node_fields(fields, after, a), FIRST)
            above.append(high)
            totals[0] = totals[0] + below[a]
            totals[3] = totals[3] - high
            for r in range(4):
                sums[r][a] = totals[r]
        for r in range(4):
            nodes = [node_fields(fields, start + r, a) for a in range(4)]
            totals = volume(nodes, SECOND)
            lower = jax.tree.map(lambda x: pltpu.roll(x, 1, 0), nodes[3])
            faces = jnp.where(number == 0, 0.0, face(lower, nodes[0], SECOND))
            totals[0] = totals[0] + faces
            totals[3] = totals[3] - pltpu.roll(faces, elements - 1, 0)
            for a in range(4):
                along = pl.ds(a, elements, stride=4)
                out[start + r, along, :] = sums[r][a] + totals[a]
        physics = base[pl.ds(pl.multiple_of(start * cols, 4 * cols), 4 * cols), :]
        physics = physics.astype(jnp.bfloat16).astype(jnp.float32).reshape(4, cols, feat)
        out[pl.ds(start, 4)] = out[pl.ds(start, 4)] + physics
        return tuple(above)

    zero = jnp.zeros((elements, feat), jnp.float32)
    lax.fori_loop(0, count, element, (zero,) * 4)


def edge_kernel(edges, early, late, from_low, from_high, partial, out, low, high, top, bottom, sems):
    col_odd_a, row_even_a, col_even_first = (early[k] for k in range(3))
    col_even_b, col_odd_b, row_even_b = (late[k] for k in range(3))
    rows, cols, feat = out.shape
    first, middle, final = pl.ds(0, 8), pl.ds(8, cols - 16), pl.ds(cols - 8, 8)
    inner = (pl.ds(1, rows - 2), middle)
    inside = pltpu.make_async_copy(partial.at[inner], out.at[inner], sems.at[4])
    inside.start()
    row, col = lax.axis_index("gx"), lax.axis_index("gy")
    place = row % WRAP
    last_row = place == WRAP - 1
    first_x = jnp.where(place < WRAP - 2, row_even_a, row_even_b)
    second_x = jnp.where(place == 0, from_low[...], from_high[...])
    even = row % 2 == 0
    west = jnp.where(even, second_x, first_x)
    east = jnp.where(even, first_x, second_x)
    first_y = jnp.where(place == 0, col_even_first, from_low[...])
    first_y = jnp.where(last_row, col_even_b, first_y)
    second_y = jnp.where(last_row, col_odd_b, col_odd_a)
    even = col % 2 == 0
    south = jnp.where(even, second_y, first_y)
    north = jnp.where(even, first_y, second_y)
    own = [primitives(edges[s]) for s in range(4)]
    west, east, south, north = (primitives(x) for x in (west, east, south, north))
    at_west = face(west, own[0], FIRST)
    at_east = -face(own[1], east, FIRST)
    at_south = face(south, own[2], SECOND)
    at_north = -face(own[3], north, SECOND)
    low[...] = partial[:, :8]
    high[...] = partial[:, cols - 8 :]
    for held, r, term in ((top, 0, at_west), (bottom, rows - 1, at_east)):
        low[r] = low[r] + term[:8]
        held[...] = partial[r, 8 : cols - 8] + term[8 : cols - 8]
        high[r] = high[r] + term[cols - 8 :]
    low[:, 0, :] = low[:, 0, :] + at_south
    high[:, 7, :] = high[:, 7, :] + at_north
    places = [
        (low, (slice(None), first)),
        (high, (slice(None), final)),
        (top, (0, middle)),
        (bottom, (rows - 1, middle)),
    ]
    writes = [
        pltpu.make_async_copy(held, out.at[p], sems.at[k]) for k, (held, p) in enumerate(places)
    ]
    for copy in writes:
        copy.start()
    for copy in writes:
        copy.wait()
    inside.wait()


def in_vmem():
    return pl.BlockSpec(memory_space=pltpu.VMEM)


def in_hbm():
    return pl.BlockSpec(memory_space=pltpu.HBM)


def anywhere():
    return pl.BlockSpec(memory_space=pl.ANY)


def kept_in_hbm(x):
    return pltpu.with_memory_space_constraint(x, pltpu.HBM)


def vmem_array(shape, dtype):
    return pltpu.VMEM(shape, dtype)


def kept_in_vmem(x):
    return pltpu.with_memory_space_constraint(x, pltpu.VMEM)


def packed(inputs, edge_map, n_x, n_y):
    rows, cols, feat = inputs[0].shape
    first = [inputs[k] for k in RESIDENT]
    return pl.pallas_call(
        functools.partial(pack_kernel, n_x, n_y),
        out_shape=[vmem_array(x.shape, x.dtype) for x in first]
        + [vmem_array((4, cols, feat), jnp.float32)]
        + [vmem_array((cols, feat), jnp.float32)] * 6,
        in_specs=[in_hbm()] * (1 + len(first)),
        out_specs=[in_vmem()] * (7 + len(first)),
        scratch_shapes=[
            pltpu.SMEM((3,) + edge_map.shape[1:], jnp.int32),
            pltpu.SemaphoreType.DMA((3 + len(first),)),
        ],
        compiler_params=pltpu.CompilerParams(vmem_limit_bytes=4 * 1024 * 1024),
        name="own_edges",
    )(*map(kept_in_hbm, (first[0], edge_map, *first[1:])))


def idle_kernel(*refs):
    pass


def nothing(count):
    def make(*edges):
        x = edges[0]
        return tuple(
            pl.pallas_call(
                idle_kernel,
                out_shape=[jax.ShapeDtypeStruct(x.shape, x.dtype)] * count,
                in_specs=[anywhere()],
                out_specs=[anywhere()] * count,
                name="no_exchange",
            )(x)
        )

    return make


def interior(early, inputs, passed, started=(), groups=()):
    air_state = inputs[0]
    held = []
    for k, x in enumerate(inputs):
        if k not in RESIDENT:
            space = pltpu.SMEM if k == 1 else pltpu.VMEM
            held.append(space(x.shape[1:] if k == 1 else x.shape, x.dtype))
    like = lambda x: vmem_array(x.shape, x.dtype)
    outs = [vmem_array(air_state.shape, jnp.float32)]
    outs += [like(x) for x in started[1:]]
    n_in, n_passed, n_started = len(inputs), len(passed), len(started)
    targets = []
    for arrays, _, number in groups:
        targets.append(len(outs) if number is None else number)
        if number is None:
            outs.append(vmem_array((len(arrays),) + arrays[0].shape, arrays[0].dtype))
    every = [x for arrays, _, _ in groups for x in arrays]
    n_fixed = len(outs)
    aliases = {n_in + k: n_fixed + k for k in range(n_passed)}
    aliases.update({n_in + n_passed + k: k for k in range(n_started)})
    rows, cols, feat = air_state.shape
    tiles = rows * cols // TILE

    def kernel(*refs):
        refs = list(refs)
        n_before = n_in + n_passed + n_started
        results = refs[n_before + len(every) :][: n_fixed + n_passed]
        rest = refs[n_before + len(every) + len(results) :]
        moved, at = [], n_before
        for (arrays, wanted, _), target in zip(groups, targets):
            moved.append((refs[at : at + len(arrays)], results[target], wanted))
            at += len(arrays)
        own = iter(rest)
        every_input = [refs[k] if k in RESIDENT else next(own) for k in range(n_in)]
        main_kernel(early, refs[:n_in], moved, results[0], (every_input, *own))

    return pl.pallas_call(
        kernel,
        out_shape=outs + [like(x) for x in passed],
        in_specs=[in_vmem() if k in RESIDENT else in_hbm() for k in range(n_in)]
        + [in_vmem()] * (n_passed + n_started)
        + [anywhere()] * len(every),
        out_specs=[in_vmem()] * (n_fixed + n_passed),
        scratch_shapes=held
        + [
            pltpu.SemaphoreType.DMA((n_in,)),
            pltpu.SemaphoreType.DMA((max(len(every), 1),)),
            pltpu.VMEM((rows * cols + TILE, feat), jnp.bfloat16),
            pltpu.VMEM((rows * cols + TILE, feat), jnp.float32),
            pltpu.SMEM((tiles + GROUP,), jnp.int32),
            pltpu.VMEM((6, rows, 4, cols // 4, feat), jnp.float32),
        ],
        input_output_aliases=aliases,
        compiler_params=pltpu.CompilerParams(vmem_limit_bytes=32 * 1024 * 1024),
        cost_estimate=pl.CostEstimate(
            flops=1_000_000_000, bytes_accessed=4_200_000, transcendentals=1_000_000
        ),
        name="columns_ahead" if early else "columns_behind",
    )(
        *(kept_in_vmem(x) if k in RESIDENT else kept_in_hbm(x) for k, x in enumerate(inputs)),
        *map(kept_in_vmem, (*passed, *started)),
        *every,
    )


def collected(arrays, wanted, passed):
    count, n_passed = len(arrays), len(passed)
    like = lambda x: vmem_array(x.shape, x.dtype)

    def kernel(*refs):
        row = lax.axis_index("gx")
        sources, target, sems = refs[:count], refs[count + n_passed], refs[-1]
        end_moves(start_moves([(sources, target, wanted)], sems, row), row)

    return pl.pallas_call(
        kernel,
        out_shape=[vmem_array((count,) + arrays[0].shape, arrays[0].dtype)]
        + [like(x) for x in passed],
        in_specs=[anywhere()] * count + [in_vmem()] * n_passed,
        out_specs=[in_vmem()] * (1 + n_passed),
        scratch_shapes=[pltpu.SemaphoreType.DMA((count,))],
        input_output_aliases={count + k: 1 + k for k in range(n_passed)},
        name="early_traces",
    )(*arrays, *map(kept_in_vmem, passed))


def boundary(edges, early, late, from_low, from_high, partial):
    rows, cols, feat = partial.shape
    return pl.pallas_call(
        edge_kernel,
        out_shape=jax.ShapeDtypeStruct(partial.shape, jnp.float32),
        in_specs=[in_vmem()] * 6,
        out_specs=in_hbm(),
        scratch_shapes=[
            pltpu.VMEM((rows, 8, feat), jnp.float32),
            pltpu.VMEM((rows, 8, feat), jnp.float32),
            pltpu.VMEM((cols - 16, feat), jnp.float32),
            pltpu.VMEM((cols - 16, feat), jnp.float32),
            pltpu.SemaphoreType.DMA((5,)),
        ],
        compiler_params=pltpu.CompilerParams(vmem_limit_bytes=8 * 1024 * 1024),
        cost_estimate=pl.CostEstimate(flops=2_000_000, bytes_accessed=600_000, transcendentals=0),
        name="boundary_faces",
    )(edges, early, late, from_low, from_high, partial)


def swap(rows, cols, n_y):
    pairs = []
    for r, other_r in rows:
        for c, other_c in cols:
            one, two = r * n_y + c, other_r * n_y + other_c
            pairs += [(one, two), (two, one)]
    return pairs


def on_device(
    air_state,
    edge_map,
    tile_class,
    in_weight,
    in_bias,
    mid_weight,
    mid_bias,
    out_weight,
    land_in,
    land_bias,
    land_out,
):
    n_x, n_y = lax.axis_size("gx"), lax.axis_size("gy")
    inputs = (
        air_state,
        tile_class,
        in_weight,
        in_bias.reshape(1, -1),
        mid_weight,
        mid_bias.reshape(1, -1),
        out_weight,
        land_in,
        land_bias.reshape(1, -1),
        land_out,
    )
    row = lax.axis_index("gx")
    late = [i for i in range(n_x) if i % WRAP == WRAP - 1]
    early = [i for i in range(n_x) if i not in late]
    first = [i for i in early if i % WRAP == 0]
    inner = [i for i in early if i not in first]
    evens = [(i, i + 1) for i in range(0, n_x, 2)]
    odds = [(i, (i + 1) % n_x) for i in range(1, n_x, 2)]
    col_evens = [(j, j + 1) for j in range(0, n_y, 2)]
    col_odds = [(j, (j + 1) % n_y) for j in range(1, n_y, 2)]
    col_same = [(j, j) for j in range(n_y)]

    def move(x, rows, cols):
        return lax.ppermute(x, ("gx", "gy"), swap(rows, cols, n_y))

    def exchange_early(col_odd, row_even):
        same = [(i, i) for i in early]
        return (
            move(col_odd, same, col_odds),
            move(row_even, [p for p in evens if p[1] not in late], col_same),
        )

    def exchange_first(col_even):
        return (move(col_even, [(i, i) for i in first], col_evens),)

    def exchange_late_cols(col_odd, col_even):
        same = [(i, i) for i in late]
        return move(col_even, same, col_evens), move(col_odd, same, col_odds)

    def exchange_late_rows(row_even):
        return (move(row_even, [p for p in evens if p[1] in late], col_same),)

    def across(x, rows, others, cols):
        pairs = [(a * n_y + j, b * n_y + j) for a, b in rows for j in range(n_y)]
        return lax.ppermute(x, ("gx", "gy"), pairs + swap(others, cols, n_y))

    place = row % WRAP
    wraps = [p for p in odds if p[0] in late]
    is_first = lambda r: r % WRAP == 0
    is_middle = lambda r: (r % WRAP > 0) & (r % WRAP < WRAP - 1)
    is_late = lambda r: r % WRAP >= WRAP - 2
    *first_inputs, own, late_even, wrap, row_even, col_even, col_odd, back = packed(
        inputs, edge_map.transpose(0, 2, 1), n_x, n_y
    )
    resident = dict(zip(RESIDENT, first_inputs))
    inputs = tuple(resident.get(k, x) for k, x in enumerate(inputs))
    partial, wrap, row_even, col_even, col_odd, back = interior(
        True, inputs, (wrap, row_even, col_even, col_odd, back)
    )
    from_low = across(wrap, wraps, [(i, i) for i in inner], col_evens)
    first_traces = lax.cond(place == 0, exchange_first, nothing(1), col_even)
    early_traces = lax.cond(place < WRAP - 1, exchange_early, nothing(2), col_odd, row_even)
    early_traces = (*early_traces, *first_traces)
    early_held, back, late_even = collected(early_traces, is_first, (back, late_even))
    from_high = across(
        back, [(b, a) for a, b in wraps], [p for p in odds if p[0] not in late], col_same
    )
    late_cols = lax.cond(
        place == WRAP - 1, exchange_late_cols, nothing(2), col_odd, col_even
    )
    late_rows = lax.cond(place >= WRAP - 2, exchange_late_rows, nothing(1), late_even)
    partial, early_held, late_held = interior(
        False,
        inputs,
        (),
        (partial, early_held),
        ((early_traces, is_middle, 1), ((*late_cols, *late_rows), is_late, None)),
    )
    return boundary(own, early_held, late_held, from_low, from_high, partial)


def solution(mesh):
    row_split, col_split = P("gx", "gy", None), P(None, "gy", None)
    return jax.shard_map(
        on_device,
        mesh=mesh,
        in_specs=(row_split, P(), col_split) + (P(),) * 8,
        out_specs=row_split,
        check_vma=False,
    )
```

```python
import functools
import math

import jax
import jax.numpy as jnp
import numpy as np
from jax import lax
from jax.experimental import pallas as pl
from jax.experimental.pallas import tpu as pltpu
from jax.sharding import PartitionSpec as P

CHUNK = 16
TILE = 64
RESIDENT = (0, 2, 3, 6)
GROUP = 8
WRAP = 8
FIRST, SECOND = "first", "second"


def lobatto_derivative():
    points = np.array([-1.0, -math.sqrt(0.2), math.sqrt(0.2), 1.0])
    barycentric = np.array(
        [1.0 / np.prod([points[j] - points[k] for k in range(4) if k != j]) for j in range(4)]
    )
    derivative = np.zeros((4, 4))
    for i in range(4):
        for j in range(4):
            if i != j:
                derivative[i, j] = barycentric[j] / barycentric[i] / (points[i] - points[j])
        derivative[i, i] = -np.sum([derivative[i, k] for k in range(4) if k != i])
    return derivative


def lane_block(shape):
    return lax.broadcasted_iota(jnp.int32, shape, len(shape) - 1) // 32


def spread(values, block, source):
    axis = values.ndim - 1
    if source == 0:
        once = jnp.where(block == 0, values, pltpu.roll(values, 32, axis))
        return jnp.where(block < 2, once, pltpu.roll(once, 64, axis))
    if source == 1:
        once = jnp.where(block == 1, values, pltpu.roll(values, 96, axis))
        return jnp.where(block < 2, once, pltpu.roll(once, 64, axis))
    once = jnp.where(block == 2, values, pltpu.roll(values, 32, axis))
    return jnp.where(block >= 2, once, pltpu.roll(once, 64, axis))


def primitives(states):
    flat = states.reshape(-1, states.shape[-1])
    block = lane_block(flat.shape)
    density = spread(flat, block, 0)
    carried = flat / density
    first = spread(carried, block, 1)
    second = spread(carried, block, 2)
    carried = jnp.where(block == 0, 1.0, carried)
    half_pressure = 0.25 * flat
    zero = jnp.zeros_like(flat)
    pressure_first = jnp.where(block == 1, pltpu.roll(half_pressure, 64, 1), zero)
    pressure_second = jnp.where(block == 2, pltpu.roll(half_pressure, 96, 1), zero)
    back = lambda x: x.reshape(states.shape)
    return {
        "q": states,
        "d": back(density),
        "c": back(carried),
        FIRST: (back(0.125 * first), back(pressure_first)),
        SECOND: (back(0.125 * second), back(pressure_second)),
    }


def pick(prims, index):
    out = {k: prims[k][index] for k in ("q", "d", "c")}
    for k in (FIRST, SECOND):
        out[k] = tuple(x[index] for x in prims[k])
    return out


def flux(one, two, axis):
    return (one["d"] + two["d"]) * (one[axis][0] + two[axis][0]) * (one["c"] + two["c"]) + (
        one[axis][1] + two[axis][1]
    )


def face(left, right, axis):
    wave = 8.0 * jnp.maximum(jnp.abs(left[axis][0]), jnp.abs(right[axis][0])) + 1.0
    return 6.0 * flux(left, right, axis) - (3.0 * wave) * (right["q"] - left["q"])


def volume(nodes, axis):
    derivative = lobatto_derivative()
    fluxes = {}
    for a in range(4):
        for b in range(a + 1, 4):
            fluxes[a, b] = fluxes[b, a] = flux(nodes[a], nodes[b], axis)
    results = []
    for a in range(4):
        total = None
        for b in range(4):
            if b != a:
                term = (-2.0 * float(derivative[a, b])) * fluxes[a, b]
                total = term if total is None else total + term
        results.append(total)
    return results


def silu(z):
    half = 0.5 * z
    return (half + half * jnp.tanh(half)).astype(jnp.bfloat16)


def dot(a, b):
    return jnp.dot(a, b, preferred_element_type=jnp.float32)


def ahead(row, col):
    return ((row % WRAP == 0) & ((row > 0) | (col > 0))) | ((row == 1) & (col == 0))


def turned(edge):
    count = edge.shape[0] // 8
    place = lax.broadcasted_iota(jnp.int32, (8, edge.shape[1]), 0)
    pieces = []
    for k in range(count):
        piece = edge[(count - 1 - k) * 8 : (count - k) * 8]
        piece = pltpu.roll(piece, 4, 0)
        piece = jnp.where(place % 4 < 2, pltpu.roll(piece, 6, 0), pltpu.roll(piece, 2, 0))
        piece = jnp.where(place % 2 < 1, pltpu.roll(piece, 7, 0), pltpu.roll(piece, 1, 0))
        pieces.append(piece)
    return jnp.concatenate(pieces, axis=0)


def pack_kernel(n_x, n_y, air_in, edge_map, *refs):
    fetched, refs = refs[: len(RESIDENT) - 1], refs[len(RESIDENT) - 1 :]
    air, *targets = refs[: len(RESIDENT)]
    own, late_even, wrap, row_even, col_even, col_odd, back, maps, sems = refs[len(RESIDENT) :]
    rows, cols, _ = air.shape
    row, col = lax.axis_index("gx"), lax.axis_index("gy")
    west, east = (row + n_x - 1) % n_x, (row + 1) % n_x
    south, north = (col + n_y - 1) % n_y, (col + 1) % n_y
    copies = [
        pltpu.make_async_copy(air_in, air, sems.at[0]),
        pltpu.make_async_copy(edge_map.at[west], maps.at[0], sems.at[1]),
        pltpu.make_async_copy(edge_map.at[row], maps.at[1], sems.at[2]),
        pltpu.make_async_copy(edge_map.at[east], maps.at[2], sems.at[3]),
    ]
    later = [
        pltpu.make_async_copy(source, target, sems.at[4 + k])
        for k, (source, target) in enumerate(zip(fetched, targets))
    ]
    for copy in copies + later:
        copy.start()
    for copy in copies:
        copy.wait()
    own[0] = air[0]
    own[1] = air[rows - 1]
    own[2] = air[:, 0, :]
    own[3] = air[:, cols - 1, :]

    def asked(code):
        edge = own[code % 4]
        return jnp.where(code >= 4, turned(edge), edge)

    to_west = asked(maps[0, 1, col])
    to_east = asked(maps[2, 0, col])
    to_south = asked(maps[1, 3, south])
    to_north = asked(maps[1, 2, north])
    even = row % 2 == 0
    row_even[...] = jnp.where(even, to_east, to_west)
    odd = jnp.where(even, to_west, to_east)
    late_even[...] = row_even[...]
    back[...] = odd
    even = col % 2 == 0
    paired = jnp.where(even, to_north, to_south)
    col_even[...] = paired
    beside = (row % WRAP == 0) | (row % WRAP == WRAP - 1)
    wrap[...] = jnp.where(beside, odd, paired)
    for copy in later:
        copy.wait()
    col_odd[...] = jnp.where(even, to_south, to_north)


def main_kernel(early, inputs, moved, result, scratch):
    held, sems, move_sems, normed, base, listed, fields = scratch
    row = lax.axis_index("gx")
    col = lax.axis_index("gy")
    moves = start_moves(moved, move_sems, row)

    @pl.when(ahead(row, col) == early)
    def _():
        copies = {}
        for k, (source, target) in enumerate(zip(inputs, held)):
            if k == 1:
                source = source.at[row]
            if k not in RESIDENT:
                copies[k] = pltpu.make_async_copy(source, target, sems.at[k])
        for k in (1, 7, 8, 4, 5, 9):
            copies[k].start()

        def ready(*numbers):
            for k in numbers:
                copies[k].wait()

        columns_and_interior(held, ready, normed, base, listed, fields, result)

    end_moves(moves, row)


def start_moves(moved, sems, row):
    moves = []
    for sources, target, wanted in moved:
        first = sum(len(copies) for copies, _ in moves)
        copies = [
            pltpu.make_async_copy(ref, target.at[k], sems.at[first + k])
            for k, ref in enumerate(sources)
        ]
        moves.append((copies, wanted))
    for copies, wanted in moves:

        @pl.when(wanted(row))
        def _():
            for copy in copies:
                copy.start()

    return moves


def end_moves(moves, row):
    for copies, wanted in moves:

        @pl.when(wanted(row))
        def _():
            for copy in copies:
                copy.wait()


def two_layers(x, weight, bias, last):
    return dot(silu(dot(x, weight[...]) + bias[...]), last[...])


def columns_and_interior(held, ready, normed_ref, base, listed, fields, out):
    air, classes, in_w, in_b, mid_w, mid_b, out_w, land_in, land_b, land_out = held
    rows, cols, feat = air.shape
    tiles = rows * cols // TILE
    chunk_cols = CHUNK * cols

    def base_chunk(c, carry):
        start = pl.multiple_of(c * CHUNK, CHUNK)
        columns = air[pl.ds(start, CHUNK)].reshape(chunk_cols, feat).astype(jnp.bfloat16)
        values = columns.astype(jnp.float32)
        mean = jnp.sum(values * values, axis=-1, keepdims=True) * (1.0 / feat)
        normed = (values * lax.rsqrt(mean + 1e-06)).astype(jnp.bfloat16)
        place = pl.ds(pl.multiple_of(c * chunk_cols, chunk_cols), chunk_cols)
        normed_ref[place, :] = normed
        base[place, :] = two_layers(normed, in_w, in_b, out_w)
        store_fields(start, CHUNK, air, fields)
        return carry

    lax.fori_loop(0, rows // CHUNK, base_chunk, 0)

    ready(1)

    def note(t, count):
        listed[count] = t
        return count + classes[0, t]

    lands = lax.fori_loop(0, tiles, note, 0)
    for k in range(GROUP):
        listed[lands + k] = tiles

    @pl.when(lands > 0)
    def _():
        ready(4, 5, 7, 8, 9)

    def land_group(first, count):
        starts = [pl.multiple_of(listed[first + k] * TILE, TILE) for k in range(count)]
        normed = jnp.concatenate([normed_ref[pl.ds(s, TILE), :] for s in starts], axis=0)
        land = silu(dot(normed, land_in[...]) + land_b[...])
        term = two_layers(land, mid_w, mid_b, land_out)
        for k, s in enumerate(starts):
            base[pl.ds(s, TILE), :] = base[pl.ds(s, TILE), :] + term[k * TILE : (k + 1) * TILE]

    def whole_group(g, carry):
        land_group(g * GROUP, GROUP)
        return carry

    half = GROUP // 2
    over = lands % GROUP
    whole = lands // GROUP + jnp.where(over > half, 1, 0)
    lax.fori_loop(0, whole, whole_group, 0)

    @pl.when((over > 0) & (over <= half))
    def _():
        land_group(whole * GROUP, half)

    interior_and_sum(air, fields, base, out)

    @pl.when(lands == 0)
    def _():
        ready(4, 5, 7, 8, 9)


def store_fields(start, count, air, fields):
    _, cols, feat = air.shape
    elements = cols // 4
    for a in range(4):
        states = air[pl.ds(start, count), pl.ds(a, elements, stride=4), :]
        flat = states.reshape(-1, feat)
        block = lane_block(flat.shape)
        density = spread(flat, block, 0)
        carried = flat * pl.reciprocal(density)
        speeds = 0.125 * carried
        half_pressure = 0.25 * flat
        values = (
            density,
            jnp.where(block == 0, 1.0, carried),
            spread(speeds, block, 1),
            spread(speeds, block, 2),
            jnp.where(block == 1, pltpu.roll(half_pressure, 64, 1), 0.0),
            jnp.where(block == 2, pltpu.roll(half_pressure, 96, 1), 0.0),
        )
        for k, value in enumerate(values):
            fields[k, pl.ds(start, count), a] = value.reshape(states.shape)


def node_fields(fields, row, a):
    d, c, u, v, p, s = (fields[k, row, a] for k in range(6))
    return {"d": d, "c": c, "q": d * c, FIRST: (u, p), SECOND: (v, s)}


def interior_and_sum(air, fields, base, out):
    rows, cols, feat = air.shape
    elements = cols // 4
    count = rows // 4
    number = lax.broadcasted_iota(jnp.int32, (elements, feat), 0)

    def element(e, below):
        start = e * 4
        after = jnp.minimum(start + 4, rows - 1)
        inside = jnp.where(e < count - 1, 1.0, 0.0)
        sums = [[None] * 4 for _ in range(4)]
        above = []
        for a in range(4):
            nodes = [node_fields(fields, start + r, a) for r in range(4)]
            totals = volume(nodes, FIRST)
            high = inside * face(nodes[3], node_fields(fields, after, a), FIRST)
            above.append(high)
            totals[0] = totals[0] + below[a]
            totals[3] = totals[3] - high
            for r in range(4):
                sums[r][a] = totals[r]
        for r in range(4):
            nodes = [node_fields(fields, start + r, a) for a in range(4)]
            totals = volume(nodes, SECOND)
            lower = jax.tree.map(lambda x: pltpu.roll(x, 1, 0), nodes[3])
            faces = jnp.where(number == 0, 0.0, face(lower, nodes[0], SECOND))
            totals[0] = totals[0] + faces
            totals[3] = totals[3] - pltpu.roll(faces, elements - 1, 0)
            for a in range(4):
                along = pl.ds(a, elements, stride=4)
                out[start + r, along, :] = sums[r][a] + totals[a]
        physics = base[pl.ds(pl.multiple_of(start * cols, 4 * cols), 4 * cols), :]
        physics = physics.astype(jnp.bfloat16).astype(jnp.float32).reshape(4, cols, feat)
        out[pl.ds(start, 4)] = out[pl.ds(start, 4)] + physics
        return tuple(above)

    zero = jnp.zeros((elements, feat), jnp.float32)
    lax.fori_loop(0, count, element, (zero,) * 4)


def edge_kernel(edges, outside, early, late, from_low, from_high, partial, out, low, high, top, bottom, sems):
    col_odd_a, col_even_first = (early[k] for k in range(2))
    row_even_a = outside[...]
    col_even_b, col_odd_b, row_even_b = (late[k] for k in range(3))
    rows, cols, feat = out.shape
    first, middle, final = pl.ds(0, 8), pl.ds(8, cols - 16), pl.ds(cols - 8, 8)
    inner = (pl.ds(1, rows - 2), middle)
    inside = pltpu.make_async_copy(partial.at[inner], out.at[inner], sems.at[4])
    inside.start()
    row, col = lax.axis_index("gx"), lax.axis_index("gy")
    place = row % WRAP
    last_row = place == WRAP - 1
    first_x = jnp.where(place < WRAP - 2, row_even_a, row_even_b)
    second_x = jnp.where(place == 0, from_low[...], from_high[...])
    even = row % 2 == 0
    west = jnp.where(even, second_x, first_x)
    east = jnp.where(even, first_x, second_x)
    first_y = jnp.where(place == 0, col_even_first, from_low[...])
    first_y = jnp.where(last_row, col_even_b, first_y)
    second_y = jnp.where(last_row, col_odd_b, col_odd_a)
    even = col % 2 == 0
    south = jnp.where(even, second_y, first_y)
    north = jnp.where(even, first_y, second_y)
    own = [primitives(edges[s]) for s in range(4)]
    west, east, south, north = (primitives(x) for x in (west, east, south, north))
    at_west = face(west, own[0], FIRST)
    at_east = -face(own[1], east, FIRST)
    at_south = face(south, own[2], SECOND)
    at_north = -face(own[3], north, SECOND)
    low[...] = partial[:, :8]
    high[...] = partial[:, cols - 8 :]
    for held, r, term in ((top, 0, at_west), (bottom, rows - 1, at_east)):
        low[r] = low[r] + term[:8]
        held[...] = partial[r, 8 : cols - 8] + term[8 : cols - 8]
        high[r] = high[r] + term[cols - 8 :]
    low[:, 0, :] = low[:, 0, :] + at_south
    high[:, 7, :] = high[:, 7, :] + at_north
    places = [
        (low, (slice(None), first)),
        (high, (slice(None), final)),
        (top, (0, middle)),
        (bottom, (rows - 1, middle)),
    ]
    writes = [
        pltpu.make_async_copy(held, out.at[p], sems.at[k]) for k, (held, p) in enumerate(places)
    ]
    for copy in writes:
        copy.start()
    for copy in writes:
        copy.wait()
    inside.wait()


def in_vmem():
    return pl.BlockSpec(memory_space=pltpu.VMEM)


def in_hbm():
    return pl.BlockSpec(memory_space=pltpu.HBM)


def anywhere():
    return pl.BlockSpec(memory_space=pl.ANY)


def kept_in_hbm(x):
    return pltpu.with_memory_space_constraint(x, pltpu.HBM)


def vmem_array(shape, dtype):
    return pltpu.VMEM(shape, dtype)


def kept_in_vmem(x):
    return pltpu.with_memory_space_constraint(x, pltpu.VMEM)


def packed(inputs, edge_map, n_x, n_y):
    rows, cols, feat = inputs[0].shape
    first = [inputs[k] for k in RESIDENT]
    return pl.pallas_call(
        functools.partial(pack_kernel, n_x, n_y),
        out_shape=[vmem_array(x.shape, x.dtype) for x in first]
        + [vmem_array((4, cols, feat), jnp.float32)]
        + [vmem_array((cols, feat), jnp.float32)] * 6,
        in_specs=[in_hbm()] * (1 + len(first)),
        out_specs=[in_vmem()] * (7 + len(first)),
        scratch_shapes=[
            pltpu.SMEM((3,) + edge_map.shape[1:], jnp.int32),
            pltpu.SemaphoreType.DMA((3 + len(first),)),
        ],
        compiler_params=pltpu.CompilerParams(vmem_limit_bytes=4 * 1024 * 1024),
        name="own_edges",
    )(*map(kept_in_hbm, (first[0], edge_map, *first[1:])))


def idle_kernel(*refs):
    pass


def nothing(count):
    def make(*edges):
        x = edges[0]
        return tuple(
            pl.pallas_call(
                idle_kernel,
                out_shape=[jax.ShapeDtypeStruct(x.shape, x.dtype)] * count,
                in_specs=[anywhere()],
                out_specs=[anywhere()] * count,
                name="no_exchange",
            )(x)
        )

    return make


def interior(early, inputs, passed, started=(), groups=()):
    air_state = inputs[0]
    held = []
    for k, x in enumerate(inputs):
        if k not in RESIDENT:
            space = pltpu.SMEM if k == 1 else pltpu.VMEM
            held.append(space(x.shape[1:] if k == 1 else x.shape, x.dtype))
    like = lambda x: vmem_array(x.shape, x.dtype)
    outs = [vmem_array(air_state.shape, jnp.float32)]
    outs += [like(x) for x in started[1:]]
    n_in, n_passed, n_started = len(inputs), len(passed), len(started)
    targets = []
    for arrays, _, number in groups:
        targets.append(len(outs) if number is None else number)
        if number is None:
            outs.append(vmem_array((len(arrays),) + arrays[0].shape, arrays[0].dtype))
    every = [x for arrays, _, _ in groups for x in arrays]
    n_fixed = len(outs)
    aliases = {n_in + k: n_fixed + k for k in range(n_passed)}
    aliases.update({n_in + n_passed + k: k for k in range(n_started)})
    rows, cols, feat = air_state.shape
    tiles = rows * cols // TILE

    def kernel(*refs):
        refs = list(refs)
        n_before = n_in + n_passed + n_started
        results = refs[n_before + len(every) :][: n_fixed + n_passed]
        rest = refs[n_before + len(every) + len(results) :]
        moved, at = [], n_before
        for (arrays, wanted, _), target in zip(groups, targets):
            moved.append((refs[at : at + len(arrays)], results[target], wanted))
            at += len(arrays)
        own = iter(rest)
        every_input = [refs[k] if k in RESIDENT else next(own) for k in range(n_in)]
        main_kernel(early, refs[:n_in], moved, results[0], (every_input, *own))

    return pl.pallas_call(
        kernel,
        out_shape=outs + [like(x) for x in passed],
        in_specs=[in_vmem() if k in RESIDENT else in_hbm() for k in range(n_in)]
        + [in_vmem()] * (n_passed + n_started)
        + [anywhere()] * len(every),
        out_specs=[in_vmem()] * (n_fixed + n_passed),
        scratch_shapes=held
        + [
            pltpu.SemaphoreType.DMA((n_in,)),
            pltpu.SemaphoreType.DMA((max(len(every), 1),)),
            pltpu.VMEM((rows * cols + TILE, feat), jnp.bfloat16),
            pltpu.VMEM((rows * cols + TILE, feat), jnp.float32),
            pltpu.SMEM((tiles + GROUP,), jnp.int32),
            pltpu.VMEM((6, rows, 4, cols // 4, feat), jnp.float32),
        ],
        input_output_aliases=aliases,
        compiler_params=pltpu.CompilerParams(vmem_limit_bytes=32 * 1024 * 1024),
        cost_estimate=pl.CostEstimate(
            flops=1_000_000_000, bytes_accessed=4_200_000, transcendentals=1_000_000
        ),
        name="columns_ahead" if early else "columns_behind",
    )(
        *(kept_in_vmem(x) if k in RESIDENT else kept_in_hbm(x) for k, x in enumerate(inputs)),
        *map(kept_in_vmem, (*passed, *started)),
        *every,
    )


def collected(arrays, wanted, passed):
    count, n_passed = len(arrays), len(passed)
    like = lambda x: vmem_array(x.shape, x.dtype)

    def kernel(*refs):
        row = lax.axis_index("gx")
        sources, target, sems = refs[:count], refs[count + n_passed], refs[-1]
        end_moves(start_moves([(sources, target, wanted)], sems, row), row)

    return pl.pallas_call(
        kernel,
        out_shape=[vmem_array((count,) + arrays[0].shape, arrays[0].dtype)]
        + [like(x) for x in passed],
        in_specs=[anywhere()] * count + [in_vmem()] * n_passed,
        out_specs=[in_vmem()] * (1 + n_passed),
        scratch_shapes=[pltpu.SemaphoreType.DMA((count,))],
        input_output_aliases={count + k: 1 + k for k in range(n_passed)},
        name="early_traces",
    )(*arrays, *map(kept_in_vmem, passed))


def boundary(edges, outside, early, late, from_low, from_high, partial):
    rows, cols, feat = partial.shape
    return pl.pallas_call(
        edge_kernel,
        out_shape=jax.ShapeDtypeStruct(partial.shape, jnp.float32),
        in_specs=[in_vmem()] * 7,
        out_specs=in_hbm(),
        scratch_shapes=[
            pltpu.VMEM((rows, 8, feat), jnp.float32),
            pltpu.VMEM((rows, 8, feat), jnp.float32),
            pltpu.VMEM((cols - 16, feat), jnp.float32),
            pltpu.VMEM((cols - 16, feat), jnp.float32),
            pltpu.SemaphoreType.DMA((5,)),
        ],
        compiler_params=pltpu.CompilerParams(vmem_limit_bytes=8 * 1024 * 1024),
        cost_estimate=pl.CostEstimate(flops=2_000_000, bytes_accessed=600_000, transcendentals=0),
        name="boundary_faces",
    )(edges, outside, early, late, from_low, from_high, partial)


def swap(rows, cols, n_y):
    pairs = []
    for r, other_r in rows:
        for c, other_c in cols:
            one, two = r * n_y + c, other_r * n_y + other_c
            pairs += [(one, two), (two, one)]
    return pairs


def on_device(
    air_state,
    edge_map,
    tile_class,
    in_weight,
    in_bias,
    mid_weight,
    mid_bias,
    out_weight,
    land_in,
    land_bias,
    land_out,
):
    n_x, n_y = lax.axis_size("gx"), lax.axis_size("gy")
    inputs = (
        air_state,
        tile_class,
        in_weight,
        in_bias.reshape(1, -1),
        mid_weight,
        mid_bias.reshape(1, -1),
        out_weight,
        land_in,
        land_bias.reshape(1, -1),
        land_out,
    )
    row = lax.axis_index("gx")
    late = [i for i in range(n_x) if i % WRAP == WRAP - 1]
    early = [i for i in range(n_x) if i not in late]
    first = [i for i in early if i % WRAP == 0]
    inner = [i for i in early if i not in first]
    evens = [(i, i + 1) for i in range(0, n_x, 2)]
    odds = [(i, (i + 1) % n_x) for i in range(1, n_x, 2)]
    col_evens = [(j, j + 1) for j in range(0, n_y, 2)]
    col_odds = [(j, (j + 1) % n_y) for j in range(1, n_y, 2)]
    col_same = [(j, j) for j in range(n_y)]

    def move(x, rows, cols):
        return lax.ppermute(x, ("gx", "gy"), swap(rows, cols, n_y))

    def exchange_early(col_odd):
        return (move(col_odd, [(i, i) for i in early], col_odds),)

    def exchange_first(col_even):
        return (move(col_even, [(i, i) for i in first], col_evens),)

    def exchange_late_cols(col_odd, col_even):
        same = [(i, i) for i in late]
        return move(col_even, same, col_evens), move(col_odd, same, col_odds)

    def exchange_late_rows(row_even):
        return (move(row_even, [p for p in evens if p[1] in late], col_same),)

    def across(x, rows, others, cols):
        pairs = [(a * n_y + j, b * n_y + j) for a, b in rows for j in range(n_y)]
        return lax.ppermute(x, ("gx", "gy"), pairs + swap(others, cols, n_y))

    place = row % WRAP
    wraps = [p for p in odds if p[0] in late]
    is_first = lambda r: r % WRAP == 0
    is_middle = lambda r: (r % WRAP > 0) & (r % WRAP < WRAP - 1)
    is_late = lambda r: r % WRAP >= WRAP - 2
    *first_inputs, own, late_even, wrap, row_even, col_even, col_odd, back = packed(
        inputs, edge_map.transpose(0, 2, 1), n_x, n_y
    )
    resident = dict(zip(RESIDENT, first_inputs))
    inputs = tuple(resident.get(k, x) for k, x in enumerate(inputs))
    partial, wrap, row_even, col_even, col_odd, back = interior(
        True, inputs, (wrap, row_even, col_even, col_odd, back)
    )
    from_low = across(wrap, wraps, [(i, i) for i in inner], col_evens)
    first_traces = lax.cond(place == 0, exchange_first, nothing(1), col_even)
    early_traces = lax.cond(place < WRAP - 1, exchange_early, nothing(1), col_odd)
    early_traces = (*early_traces, *first_traces)
    outside = move(row_even, [p for p in evens if p[1] not in late], col_same)
    early_held, back, late_even = collected(early_traces, is_first, (back, late_even))
    from_high = across(
        back, [(b, a) for a, b in wraps], [p for p in odds if p[0] not in late], col_same
    )
    late_cols = lax.cond(
        place == WRAP - 1, exchange_late_cols, nothing(2), col_odd, col_even
    )
    late_rows = lax.cond(place >= WRAP - 2, exchange_late_rows, nothing(1), late_even)
    partial, early_held, late_held = interior(
        False,
        inputs,
        (),
        (partial, early_held),
        ((early_traces, is_middle, 1), ((*late_cols, *late_rows), is_late, None)),
    )
    return boundary(own, outside, early_held, late_held, from_low, from_high, partial)


def solution(mesh):
    row_split, col_split = P("gx", "gy", None), P(None, "gy", None)
    return jax.shard_map(
        on_device,
        mesh=mesh,
        in_specs=(row_split, P(), col_split) + (P(),) * 8,
        out_specs=row_split,
        check_vma=False,
    )
```
